256 devices in a mesh: section: 16 (over y_hi, z), head: 4 (over y_lo, core), page: 4 (over x).
Axes of the slice: x: 4, y: 4 (y_hi: 2, y_lo: 2; y = y_hi * 2 + y_lo), z: 8, core: 2. Of those that a mesh axis runs over, the one named last changes fastest.
Arguments:
- grad_in: float32 [16, 64, 3072], P('section', None, 'page'), may hold values from -6 to 6
- grad_fresh: float32 [64, 3072], P(None, 'page'), may hold values from -6 to 6
- queries: float32 [16, 2, 64, 3072], P('section', None, None, 'head'), may hold values from -320 to 320
- key_cache: float32 [16, 2048, 1024], P('section', 'page', 'head'), may hold values from -6 to 6
- value_cache: float32 [16, 2048, 1024], P('section', 'page', 'head'), may hold values from -6 to 6
- key_fresh: float32 [2048, 1024], P('page', 'head'), may hold values from -6 to 6
- value_fresh: float32 [2048, 1024], P('page', 'head'), may hold values from -6 to 6
- key_grad_in: float32 [16, 2048, 1024], P('section', 'page', 'head'), may hold values from -4 to 4
- value_grad_in: float32 [16, 2048, 1024], P('section', 'page', 'head'), may hold values from -4 to 4
- page_table: int32 [16, 16], P('section'), may hold values from 0 to 15, as said below
- offsets: int32 [16], P('section'), may hold values from 0 to 1984
- page_fresh: int32 [16], replicated, may hold values from 0 to 15, as said below
- offset_fresh: int32 [1], replicated, may hold values from 0 to 1984
- w_query: float32 [16, 3072, 3072], P('section', 'page', 'head'), may hold values from -0.109375 to 0.109375
- w_out: float32 [16, 3072, 3072], P('section', 'head', 'page'), may hold values from -0.109375 to 0.109375
Outputs:
- grad_next: float32 [16, 64, 3072], P('section', None, 'page')
- key_grad_next: float32 [16, 2048, 1024], P('section', 'page', 'head')
- value_grad_next: float32 [16, 2048, 1024], P('section', 'page', 'head')
The draws below stay inside these ranges and needn't reach their ends.
Inputs may be any that keep to these rules, and one draw needn't show every extreme that they name: `page_table`: each row is a permutation of 0 to 15: entry b is the logical block held in physical rows b * 128 to (b + 1) * 128 - 1. `page_fresh`: A permutation of 0 to 15, read as page_table's rows.
All inputs are finite; a program needn't handle non-finite values.
Results may differ from the reference program's by a relative error of at most 0.0003.
Values sent between devices are 32-bit elements; how exact they have to be, the bound alone decides.
No kernel may reach another device: no remote copies, remote signals or barrier semaphores. Data moves between devices by JAX's collectives and lax.ppermute only.
A program may use at most 64 MiB of HBM per device.

```python
import jax
import jax.numpy as jnp
from jax import lax

D = 3072
HQ = 24
KVH = 8
HD = 128
QROWS = 64
KVROWS = 2048
BLOCK = 128
NBLK = 16
SECTIONS = 16


def tables_every(key):
    base = jax.random.fold_in(key, 101)

    def single(index):
        return jax.random.permutation(jax.random.fold_in(base, index), NBLK).astype(jnp.int32)
    return jax.vmap(single)(jnp.arange(SECTIONS + 1))


def quiet_channels(key):
    base = jax.random.fold_in(key, 404)

    def single(index):
        return jax.random.permutation(jax.random.fold_in(base, index), HD) < HD // 2
    return jax.vmap(single)(jnp.arange(KVH))


def keys_every(key):
    base = jax.random.fold_in(key, 202)
    raw_keys = jax.random.truncated_normal(base, -6.0, 6.0, (SECTIONS + 1, KVROWS, KVH * HD), jnp.float32)
    quiet = quiet_channels(key).reshape(KVH * HD)
    raw_keys = raw_keys * jnp.where(quiet, 0.03, 1.0).astype(jnp.float32)[None, None, :]
    return raw_keys


def draw_key_cache(key, part):
    return keys_every(key)[:SECTIONS]


def draw_key_fresh(key, part):
    return keys_every(key)[SECTIONS]


def draw_page_table(key, part):
    return tables_every(key)[:SECTIONS]


def draw_page_fresh(key, part):
    return tables_every(key)[SECTIONS]


def draw_queries(key, part):
    quiet = jnp.repeat(quiet_channels(key), HQ // KVH, axis=0).reshape(HQ * HD)
    key = jax.random.fold_in(key, 303)
    loud_part = 2.0 * jax.random.truncated_normal(jax.random.fold_in(key, 1), -6.0, 6.0, (SECTIONS, 2, QROWS, HQ * HD), jnp.float32)
    quiet_part = 20.0 * jax.random.truncated_normal(jax.random.fold_in(key, 2), -8.0, 8.0, (SECTIONS, 2, QROWS, HQ * HD), jnp.float32)
    raw_queries = jnp.where(quiet[None, None, None, :], quiet_part, loud_part)
    return raw_queries


def plant(entries, stream_key, low, top_value):
    longest = entries.shape.index(max(entries.shape))
    spots = []
    for shift in (0, 1):
        where = [jax.random.randint(jax.random.fold_in(stream_key, axis), (), 0, length) for axis, length in enumerate(entries.shape)]
        where[longest] = (where[longest] + shift) % entries.shape[longest]
        spots.append(tuple(where))
    return entries.at[spots[0]].set(low).at[spots[1]].set(top_value)


def block_levels(own_key, shape, pieces, smallest, top_value):
    level = 1.0
    for dim, shards_of in pieces:
        draws = jax.random.uniform(jax.random.fold_in(jax.random.fold_in(own_key, 6), dim), (shards_of,), jnp.float32, smallest / len(pieces), top_value / len(pieces))
        level = level * jnp.repeat(jnp.exp(draws), shape[dim] // shards_of).reshape((-1,) + (1,) * (len(shape) - 1 - dim))
    return level


def gaussian(stream_key, dims, scale, limit, split=(), held_as=jnp.bfloat16):
    result = scale * jax.random.normal(stream_key, dims, jnp.float32)
    if split:
        result = result * block_levels(stream_key, dims, split, -0.22, 0.18)
    return jnp.clip(result, -limit, limit).astype(held_as)


def setup_inputs(seed: int = 0) -> dict:
    streams_of = jax.random.split(jax.random.key(seed), 16)
    return {
        "grad_in": gaussian(streams_of[0], (SECTIONS, QROWS, D), 1.0, 6.0, ((0, 16), (2, 4)), jnp.float32),
        "grad_fresh": gaussian(streams_of[1], (QROWS, D), 1.0, 6.0, ((1, 4),), jnp.float32),
        "queries": draw_queries(jax.random.fold_in(streams_of[15], 71), 0),
        "key_cache": draw_key_cache(jax.random.fold_in(streams_of[15], 71), 0),
        "value_cache": gaussian(streams_of[4], (SECTIONS, KVROWS, KVH * HD), 1.0, 6.0, ((0, 16), (1, 4), (2, 4)), jnp.float32),
        "key_fresh": draw_key_fresh(jax.random.fold_in(streams_of[15], 71), 0),
        "value_fresh": gaussian(streams_of[6], (KVROWS, KVH * HD), 1.0, 6.0, ((0, 4), (1, 4)), jnp.float32),
        "key_grad_in": gaussian(streams_of[7], (SECTIONS, KVROWS, KVH * HD), 0.3, 4.0, ((0, 16), (1, 4), (2, 4)), jnp.float32),
        "value_grad_in": gaussian(streams_of[8], (SECTIONS, KVROWS, KVH * HD), 0.3, 4.0, ((0, 16), (1, 4), (2, 4)), jnp.float32),
        "page_table": draw_page_table(jax.random.fold_in(streams_of[15], 71), 0),
        "offsets": plant(jax.random.randint(streams_of[10], (SECTIONS,), 0, KVROWS - QROWS + 1), jax.random.fold_in(streams_of[10], 1), 0, KVROWS - QROWS).astype(jnp.int32),
        "page_fresh": draw_page_fresh(jax.random.fold_in(streams_of[15], 71), 0),
        "offset_fresh": jax.random.randint(streams_of[12], (1,), 0, KVROWS - QROWS + 1).astype(jnp.int32),
        "w_query": gaussian(streams_of[13], (SECTIONS, D, HQ * HD), D ** -0.5, 0.109375, ((0, 16), (1, 4), (2, 4)), jnp.float32),
        "w_out": gaussian(streams_of[14], (SECTIONS, HQ * HD, D), (HQ * HD) ** -0.5, 0.109375, ((0, 16), (1, 4), (2, 4)), jnp.float32),
    }


precise = lax.Precision.HIGHEST


def layer_backward(incoming, saved_query, key_block, value_block, table_row, offset_now, w_query_layer, w_out_layer, key_sum, value_sum):
    query_count = saved_query.shape[0]
    key_count = key_block.shape[0]
    shared = key_block.shape[1] // HD
    heads_here = saved_query.shape[1] // HD
    group_size = heads_here // shared
    score_scale = HD ** -0.5
    d_out = jnp.einsum("qc,hc->qh", incoming, w_out_layer, precision=precise)
    block_count = key_count // BLOCK
    positions = jnp.repeat(table_row, BLOCK) * BLOCK + jnp.tile(jnp.arange(BLOCK, dtype=jnp.int32), block_count)
    visible = positions[None, :] <= offset_now + jnp.arange(query_count, dtype=jnp.int32)[:, None]
    query_heads = saved_query.reshape(query_count, shared, group_size, HD)
    key_heads = key_block.reshape(key_count, shared, HD)
    value_heads = value_block.reshape(key_count, shared, HD)
    scores = jnp.einsum("qgrd,kgd->grqk", query_heads, key_heads, precision=precise) * score_scale
    masked = jnp.where(visible, scores, -1e30)
    row_top = jnp.max(masked, axis=-1, keepdims=True)
    weights_raw = jnp.where(visible, jnp.exp(masked - row_top), 0.0)
    row_total = jnp.sum(weights_raw, axis=-1, keepdims=True)
    probs = weights_raw / row_total
    attended = jnp.einsum("grqk,kgd->qgrd", probs, value_heads, precision=precise)
    dout_heads = d_out.reshape(query_count, shared, group_size, HD)
    delta = jnp.sum(dout_heads * attended, axis=-1).transpose(1, 2, 0)[..., None]
    d_prob = jnp.einsum("qgrd,kgd->grqk", dout_heads, value_heads, precision=precise)
    d_score = probs * (d_prob - delta)
    d_query = jnp.einsum("grqk,kgd->qgrd", d_score, key_heads, precision=precise).reshape(query_count, heads_here * HD) * score_scale
    key_step = jnp.einsum("grqk,qgrd->kgd", d_score, query_heads, precision=precise).reshape(key_count, shared * HD) * score_scale
    value_step = jnp.einsum("grqk,qgrd->kgd", probs, dout_heads, precision=precise).reshape(key_count, shared * HD)
    d_input = incoming + jnp.einsum("qh,ch->qc", d_query, w_query_layer, precision=precise)
    return d_input, key_sum + key_step, value_sum + value_step


def reference(grad_in, grad_fresh, queries, key_cache, value_cache, key_fresh, value_fresh, key_grad_in, value_grad_in, page_table, offsets, page_fresh, offset_fresh, w_query, w_out):
    carried = [None]
    for section_index in range(1, SECTIONS):
        carried.append(layer_backward(grad_in[section_index], queries[section_index, 0], key_cache[section_index], value_cache[section_index], page_table[section_index], offsets[section_index], w_query[section_index], w_out[section_index], key_grad_in[section_index], value_grad_in[section_index]))
    grad_list = []
    key_list = []
    value_list = []
    for section_index in range(SECTIONS):
        if section_index + 1 < SECTIONS:
            incoming, key_start, value_start = carried[section_index + 1]
            key_block = key_cache[section_index + 1]
            value_block = value_cache[section_index + 1]
            table_row = page_table[section_index + 1]
            offset_now = offsets[section_index + 1]
        else:
            incoming = grad_fresh
            key_start = jnp.zeros_like(key_fresh)
            value_start = jnp.zeros_like(value_fresh)
            key_block = key_fresh
            value_block = value_fresh
            table_row = page_fresh
            offset_now = offset_fresh[0]
        d_input, key_total, value_total = layer_backward(incoming, queries[section_index, 1], key_block, value_block, table_row, offset_now, w_query[section_index], w_out[section_index], key_start, value_start)
        grad_list.append(d_input)
        key_list.append(key_total)
        value_list.append(value_total)
    return jnp.stack(grad_list), jnp.stack(key_list), jnp.stack(value_list)
```

```python
import functools

import jax
import jax.numpy as jnp
from jax import lax
from jax.experimental import pallas as pl
from jax.experimental.pallas import tpu as pltpu
from jax.sharding import PartitionSpec as P

HD = 128
BLOCK = 128
Q = 64
HALF = Q // 2
KEYS = 512
KV = 2
GROUP = 3
ROWS = GROUP * Q
WIDE = KV * GROUP * HD
SCALE = HD ** (-0.5)
F32 = jnp.float32
BF16 = jnp.bfloat16
NN = (((1,), (0,)), ((), ()))
NT = (((1,), (1,)), ((), ()))


def split(x):
    high = x.astype(BF16)
    return high, (x - high.astype(F32)).astype(BF16)


def dot(a, b, dims):
    return lax.dot_general(a, b, dims, preferred_element_type=F32)


def dot3(a, b, dims):
    (a_high, a_low), (b_high, b_low) = a, b
    return dot(a_high, b_high, dims) + (dot(a_low, b_high, dims) + dot(a_high, b_low, dims))


def stacked(x, g):
    return jnp.concatenate([x[:, (g * GROUP + r) * HD : (g * GROUP + r + 1) * HD] for r in range(GROUP)], 0)


def spread(groups):
    return jnp.concatenate([groups[g][r * Q : (r + 1) * Q] for g in range(KV) for r in range(GROUP)], 1)


def as_columns(row):
    return jnp.transpose(jnp.broadcast_to(row, (HD, ROWS)))


def call(body, outs, *args, scratch=(), mb=24, smem=()):
    in_specs = [
        pl.BlockSpec(memory_space=pltpu.SMEM if i in smem else pltpu.VMEM) for i in range(len(args))
    ]
    return pl.pallas_call(
        body,
        out_shape=[jax.ShapeDtypeStruct(s, d) for s, d in outs],
        in_specs=in_specs,
        out_specs=[pl.BlockSpec(memory_space=pltpu.VMEM)] * len(outs),
        scratch_shapes=scratch,
        compiler_params=pltpu.CompilerParams(vmem_limit_bytes=mb << 20),
    )(*args)


def dout_first_body(g_ref, w_ref, top_ref, bottom_ref, high_ref, low_ref):
    g = split(g_ref[...])
    w = split(w_ref[...])
    high_ref[...], low_ref[...] = w
    part = dot3(g, w, NT)
    top_ref[...] = part[:HALF]
    bottom_ref[...] = part[HALF:]


def dout_first(g, w):
    tile = 256
    count = w.shape[0] // tile
    half = pl.BlockSpec((HALF, tile), lambda i: (0, i))
    rows = pl.BlockSpec((tile, WIDE), lambda i: (i, 0))
    return pl.pallas_call(
        dout_first_body,
        grid=(count,),
        out_shape=[jax.ShapeDtypeStruct((HALF, WIDE), F32)] * 2 + [jax.ShapeDtypeStruct(w.shape, BF16)] * 2,
        in_specs=[pl.BlockSpec((Q, WIDE), lambda i: (0, 0)), rows],
        out_specs=[half, half, rows, rows],
        compiler_params=pltpu.CompilerParams(vmem_limit_bytes=24 << 20),
    )(g, w)


def dout_second_body(mine_ref, other_ref, fresh_ref, high_ref, low_ref, top_ref, bottom_ref, g_ref):
    core = lax.axis_index("head") % 2
    final = lax.axis_index("section") == lax.axis_size("section") - 1
    mine, other = mine_ref[...], other_ref[...]
    top = jnp.where(core == 0, mine, other)
    bottom = jnp.where(core == 0, other, mine)
    g = jnp.where(final, fresh_ref[...], jnp.concatenate([top, bottom], 0))
    g_ref[...] = g
    part = dot3(split(g), (high_ref[...], low_ref[...]), NT)
    top_ref[...] = part[:HALF]
    bottom_ref[...] = part[HALF:]


def dout_second(mine, other, fresh, high, low):
    half = ((HALF, WIDE), F32)
    return call(dout_second_body, [half, half, ((Q, WIDE), F32)], mine, other, fresh, high, low)


def split_body(w_ref, high_ref, low_ref):
    high_ref[...], low_ref[...] = split(w_ref[...])


def split_weights(w):
    tile = 256
    rows = pl.BlockSpec((tile, w.shape[1]), lambda i: (i, 0))
    return pl.pallas_call(
        split_body,
        grid=(w.shape[0] // tile,),
        out_shape=[jax.ShapeDtypeStruct(w.shape, BF16)] * 2,
        in_specs=[rows],
        out_specs=[rows, rows],
        compiler_params=pltpu.CompilerParams(vmem_limit_bytes=24 << 20),
    )(w)


def scores_body(q_ref, k_ref, table_ref, s_ref, top_ref):
    page = lax.axis_index("page")
    offset = table_ref[16]
    query = lax.broadcasted_iota(jnp.int32, (BLOCK, ROWS), 1) % Q
    key = lax.broadcasted_iota(jnp.int32, (BLOCK, ROWS), 0)
    top_ref[...] = jnp.zeros_like(top_ref)
    for g in range(KV):
        s = lax.dot_general(
            k_ref[:, g * HD : (g + 1) * HD],
            stacked(q_ref[...], g),
            NT,
            precision=lax.Precision.HIGHEST,
            preferred_element_type=F32,
        ) * SCALE
        best = None
        for b in range(KEYS // BLOCK):
            start = table_ref[page * (KEYS // BLOCK) + b] * BLOCK
            seen = start + key <= offset + query
            block = jnp.where(seen, s[b * BLOCK : (b + 1) * BLOCK], -1e30)
            s_ref[g, b * BLOCK : (b + 1) * BLOCK] = block
            most = jnp.max(block, axis=0, keepdims=True)
            best = most if best is None else jnp.maximum(best, most)
        top_ref[g : g + 1, :ROWS] = best


def scores(q, k, table):
    return call(scores_body, [((KV, KEYS, ROWS), F32), ((8, 256), F32)], q, k, table, smem=(2,))


def weights_body(s_ref, t0, t1, t2, t3, k_ref, v_ref, e_ref, top_ref, bottom_ref, kt_high, kt_low, v_high, v_low):
    best = jnp.maximum(jnp.maximum(t0[...], t1[...]), jnp.maximum(t2[...], t3[...]))
    v_high[...], v_low[...] = split(v_ref[...])
    groups, totals = [], []
    for g in range(KV):
        e = jnp.exp(s_ref[g] - best[g : g + 1, :ROWS])
        e_ref[g] = e
        totals.append(jnp.sum(e, axis=0, keepdims=True))
        kt = split(jnp.transpose(k_ref[:, g * HD : (g + 1) * HD]))
        kt_high[g], kt_low[g] = kt
        groups.append(jnp.transpose(dot3(kt, split(e), NN)))
    b = spread(groups)
    top_ref[:HALF] = b[:HALF]
    top_ref[HALF:] = jnp.zeros((8, WIDE), F32)
    for g in range(KV):
        top_ref[HALF + g : HALF + g + 1, :ROWS] = totals[g]
    bottom_ref[...] = b[HALF:]


def weights(s, tops, k, v):
    return call(
        weights_body,
        [
            ((KV, KEYS, ROWS), F32),
            ((HALF + 8, WIDE), F32),
            ((HALF, WIDE), F32),
            ((KV, HD, KEYS), BF16),
            ((KV, HD, KEYS), BF16),
            ((KEYS, KV * HD), BF16),
            ((KEYS, KV * HD), BF16),
        ],
        s, *tops, k, v,
    )


def products_body(d0, d1, d2, d3, e_ref, kt_high, kt_low, v_high, v_low, dp_ref, top_ref, bottom_ref, dout_ref):
    dout = jnp.concatenate([d0[...] + d1[...], d2[...] + d3[...]], 0)
    dout_ref[...] = dout
    groups, deltas = [], []
    for g in range(KV):
        cols = slice(g * HD, (g + 1) * HD)
        dp = dot3((v_high[:, cols], v_low[:, cols]), split(stacked(dout, g)), NT)
        dp_ref[g] = dp
        x = e_ref[g] * dp
        deltas.append(jnp.sum(x, axis=0, keepdims=True))
        groups.append(jnp.transpose(dot3((kt_high[g], kt_low[g]), split(x), NN)))
    a = spread(groups)
    top_ref[:HALF] = a[:HALF]
    top_ref[HALF:] = jnp.zeros((8, WIDE), F32)
    for g in range(KV):
        top_ref[HALF + g : HALF + g + 1, :ROWS] = deltas[g]
    bottom_ref[...] = a[HALF:]


def products(dout, e, kt_high, kt_low, v_high, v_low):
    return call(
        products_body,
        [((KV, KEYS, ROWS), F32), ((HALF + 8, WIDE), F32), ((HALF, WIDE), F32), ((Q, WIDE), F32)],
        *dout, e, kt_high, kt_low, v_high, v_low,
    )


def input_body(a0, a1, a2, a3, b0, b1, b2, b3, g_ref, high_ref, low_ref, keep_ref, send_ref):
    head = lax.axis_index("head")
    a_top, b_top = a0[...] + a1[...], b0[...] + b1[...]
    a = jnp.concatenate([a_top[:HALF], a2[...] + a3[...]], 0)
    b = jnp.concatenate([b_top[:HALF], b2[...] + b3[...]], 0)
    groups = []
    for g in range(KV):
        total = b_top[HALF + g : HALF + g + 1, :ROWS]
        delta = a_top[HALF + g : HALF + g + 1, :ROWS] / total
        groups.append((stacked(a, g) - as_columns(delta) * stacked(b, g)) * as_columns(SCALE / total))
    part = dot3(split(spread(groups)), (high_ref[...], low_ref[...]), NT)
    part = part + jnp.where(head == 0, g_ref[...], 0.0)
    first = head % 2 == 0
    keep_ref[...] = jnp.where(first, part[:HALF], part[HALF:])
    send_ref[...] = jnp.where(first, part[HALF:], part[:HALF])


def input_gradient(a, b, g, high, low):
    half = ((HALF, WIDE), F32)
    return call(input_body, [half, half], *a, *b, g, high, low)


def sums_body(a0, a1, b0, b1, e_ref, dp_ref, dout_ref, q_ref, key_ref, value_ref, key_out, value_out):
    a_top, b_top = a0[HALF:] + a1[HALF:], b0[HALF:] + b1[HALF:]
    for g in range(KV):
        total = b_top[g : g + 1, :ROWS]
        delta = a_top[g : g + 1, :ROWS] / total
        probs = e_ref[g] * (1.0 / total)
        d_score = probs * (dp_ref[g] - delta)
        cols = slice(g * HD, (g + 1) * HD)
        value_out[:, cols] = value_ref[:, cols] + dot3(split(probs), split(stacked(dout_ref[...], g)), NN)
        key_out[:, cols] = key_ref[:, cols] + SCALE * dot3(split(d_score), split(stacked(q_ref[...], g)), NN)


def gradient_sums(a, b, e, dp, dout, q, key_sum, value_sum):
    cache = ((KEYS, KV * HD), F32)
    return call(sums_body, [cache, cache], a[0], a[1], b[0], b[1], e, dp, dout, q, key_sum, value_sum)


def swap(bits, n=4):
    return [(i, i ^ bits) for i in range(n)]


def page_sum(top, bottom):
    top = top + lax.ppermute(top, "page", swap(1))
    bottom = bottom + lax.ppermute(bottom, "page", swap(3))
    return (top, lax.ppermute(top, "page", swap(3)), bottom, lax.ppermute(bottom, "page", swap(1)))


def page_all(x):
    return [x] + [lax.ppermute(x, "page", [(i, (i + d) % 4) for i in range(4)]) for d in (1, 2, 3)]


def back(flip=0):
    heads = 4
    return [
        (s * heads + h, (s - 1) * heads + (h ^ flip)) for s in range(1, 16) for h in range(heads)
    ]


def tied(value, after):
    return lax.optimization_barrier((value, after))[0]


def per_device(
    grad_in, grad_fresh, queries, key_cache, value_cache, key_fresh, value_fresh, key_grad_in, value_grad_in,
    page_table, offsets, page_fresh, offset_fresh, w_query, w_out,
):
    is_final = lax.axis_index("section") == lax.axis_size("section") - 1
    both = ("section", "head")
    g1, q1, q2 = grad_in[0], queries[0, 0], queries[0, 1]
    k1, v1 = key_cache[0], value_cache[0]
    pad = jnp.zeros((111,), jnp.int32)
    table1 = jnp.concatenate([page_table[0], offsets, pad])
    table_fresh = jnp.concatenate([page_fresh, offset_fresh, pad])

    top, bottom, wo_high, wo_low = dout_first(g1, w_out[0])
    dout1 = page_sum(top, bottom)
    s1, m1 = scores(q1, k1, table1)
    tops1 = page_all(m1)
    e1, b_top, b_bottom, *splits1 = weights(s1, tops1, k1, v1)
    b1 = page_sum(b_top, b_bottom)
    wq_high, wq_low = split_weights(w_query[0])

    back_section = [(i, i - 1) for i in range(1, 16)]
    table2 = jnp.where(is_final, table_fresh, lax.ppermute(table1, "section", back_section))
    k2 = jnp.where(is_final, key_fresh, lax.ppermute(k1, "section", back_section))
    v2 = jnp.where(is_final, value_fresh, lax.ppermute(v1, "section", back_section))

    dp1, a_top, a_bottom, dout1 = products(dout1, e1, *splits1)
    a1 = page_sum(a_top, a_bottom)
    keep, send = input_gradient(a1, b1, g1, wq_high, wq_low)
    part = keep + lax.ppermute(send, "head", swap(1))
    mine = lax.ppermute(part, both, back()) + lax.ppermute(part, both, back(2))
    other = lax.ppermute(mine, "head", swap(1))
    key_sum, value_sum = gradient_sums(a1, b1, e1, dp1, dout1, q1, key_grad_in[0], value_grad_in[0])
    key_sum, value_sum = tied((key_sum, value_sum), mine)
    key_sum = lax.ppermute(key_sum, "section", back_section)
    value_sum = lax.ppermute(value_sum, "section", back_section)

    s2, m2 = scores(q2, k2, table2)
    tops2 = page_all(m2)
    e2, b_top, b_bottom, *splits2 = weights(s2, tops2, k2, v2)
    b2 = page_sum(b_top, b_bottom)

    top, bottom, g2 = dout_second(mine, other, grad_fresh, wo_high, wo_low)
    dout2 = page_sum(top, bottom)
    dp2, a_top, a_bottom, dout2 = products(dout2, e2, *splits2)
    a2 = page_sum(a_top, a_bottom)
    keep, send = input_gradient(a2, b2, g2, wq_high, wq_low)
    part = keep + lax.ppermute(send, "head", swap(1))
    mine = part + lax.ppermute(part, "head", swap(2))
    other = lax.ppermute(mine, "head", swap(1))
    first = lax.axis_index("head") % 2 == 0
    grad_done = jnp.concatenate([jnp.where(first, mine, other), jnp.where(first, other, mine)], 0)
    key_final, value_final = gradient_sums(a2, b2, e2, dp2, dout2, q2, key_sum, value_sum)
    return (grad_done[None], key_final[None], value_final[None])


def solution(mesh):
    placed = (
        P("section", None, "page"),
        P(None, "page"),
        P("section", None, None, "head"),
        P("section", "page", "head"),
        P("section", "page", "head"),
        P("page", "head"),
        P("page", "head"),
        P("section", "page", "head"),
        P("section", "page", "head"),
        P("section", None),
        P("section"),
        P(),
        P(),
        P("section", "page", "head"),
        P("section", "head", "page"),
    )
    return jax.shard_map(
        per_device,
        mesh=mesh,
        in_specs=placed,
        out_specs=(
            P("section", None, "page"),
            P("section", "page", "head"),
            P("section", "page", "head"),
        ),
        check_vma=False,
    )
```

```python
import functools

import jax
import jax.numpy as jnp
from jax import lax
from jax.experimental import pallas as pl
from jax.experimental.pallas import tpu as pltpu
from jax.sharding import PartitionSpec as P

HD = 128
BLOCK = 128
Q = 64
HALF = Q // 2
FRONT_MB = 60
TAIL = 8
KEYS = 512
KV = 2
GROUP = 3
ROWS = GROUP * Q
WIDE = KV * GROUP * HD
SCALE = HD ** (-0.5)
F32 = jnp.float32
BF16 = jnp.bfloat16
NN = (((1,), (0,)), ((), ()))
NT = (((1,), (1,)), ((), ()))


def split(x):
    high = x.astype(BF16)
    return high, (x - high.astype(F32)).astype(BF16)


def dot(a, b, dims):
    return lax.dot_general(a, b, dims, preferred_element_type=F32)


def dot3(a, b, dims):
    (a_high, a_low), (b_high, b_low) = a, b
    return dot(a_high, b_high, dims) + (dot(a_low, b_high, dims) + dot(a_high, b_low, dims))


def stacked(x, g):
    return jnp.concatenate([x[:, (g * GROUP + r) * HD : (g * GROUP + r + 1) * HD] for r in range(GROUP)], 0)


def spread(groups):
    return jnp.concatenate([groups[g][r * Q : (r + 1) * Q] for g in range(KV) for r in range(GROUP)], 1)


def as_columns(row):
    return jnp.transpose(jnp.broadcast_to(row, (HD, ROWS)))


def call(body, outs, *args, scratch=(), mb=6, smem=(), free=()):
    spaces = [pltpu.SMEM if i in smem else pl.ANY if i in free else pltpu.VMEM for i in range(len(args))]
    return pl.pallas_call(
        body,
        out_shape=[jax.ShapeDtypeStruct(s, d) for s, d in outs],
        in_specs=[pl.BlockSpec(memory_space=space) for space in spaces],
        out_specs=[pl.BlockSpec(memory_space=pltpu.VMEM)] * len(outs),
        scratch_shapes=scratch,
        cost_estimate=pl.CostEstimate(flops=0, bytes_accessed=0, transcendentals=0),
        compiler_params=pltpu.CompilerParams(vmem_limit_bytes=mb << 20),
    )(*args)


SCORES = ((KV, KEYS, ROWS), F32)
CACHE = ((KEYS, KV * HD), F32)
FULL = ((Q, WIDE), F32)
PIECE = ((HALF, WIDE), F32)
WITH_ROWS = ((Q + TAIL, WIDE), F32)
STATS = ((TAIL, WIDE), F32)
PACK = ((2 * KEYS + TAIL, KV * HD), F32)
WEIGHT = ((WIDE, WIDE), BF16)
KEYS_T = ((KV, HD, KEYS), BF16)
CACHE_BF = ((KEYS, KV * HD), BF16)


def limits(table_ref, offset_ref):
    page = lax.axis_index("page")
    rows = []
    for b in range(8):
        bound = offset_ref[0] - table_ref[page * 4 + b % 4] * BLOCK
        rows.append(jnp.full((1, KV * HD), bound, jnp.int32).astype(F32))
    return jnp.concatenate(rows, 0)


def masked_scores(g, q, k, bounds, s_ref):
    lead = (
        lax.broadcasted_iota(jnp.int32, (BLOCK, ROWS), 0) - lax.broadcasted_iota(jnp.int32, (BLOCK, ROWS), 1) % Q
    ).astype(F32)
    s = lax.dot_general(
        k, stacked(q, g), NT, precision=lax.Precision.HIGHEST, preferred_element_type=F32
    ) * SCALE
    best = None
    for b in range(KEYS // BLOCK):
        block = jnp.where(lead <= bounds[b : b + 1, :ROWS], s[b * BLOCK : (b + 1) * BLOCK], -1e30)
        s_ref[g, b * BLOCK : (b + 1) * BLOCK] = block
        most = jnp.max(block, axis=0, keepdims=True)
        best = most if best is None else jnp.maximum(best, most)
    return best


def front_body(
    q_hbm, k_hbm, v_hbm, g_hbm, w_hbm, table_ref, offset_ref, fresh_table_ref, fresh_offset_ref,
    s_ref, part_ref, pack_hbm, fresh_ref,
    q_ref, pack_ref, g_ref, w_ref, sems,
):
    count = 3
    tile = WIDE // count
    copies = [
        pltpu.make_async_copy(q_hbm.at[0, 0], q_ref, sems.at[0]),
        pltpu.make_async_copy(k_hbm.at[0], pack_ref.at[pl.ds(0, KEYS)], sems.at[1]),
        pltpu.make_async_copy(g_hbm.at[0], g_ref, sems.at[2]),
    ]
    for i in range(count):
        part = pl.ds(i * tile, tile)
        copies.append(pltpu.make_async_copy(w_hbm.at[0, part], w_ref.at[part], sems.at[3 + i]))
    for copy in copies:
        copy.start()
    load = pltpu.make_async_copy(v_hbm.at[0], pack_ref.at[pl.ds(KEYS, KEYS)], sems.at[3 + count])
    load.start()
    bounds = limits(table_ref, offset_ref)
    pack_ref[2 * KEYS :] = bounds
    fresh_ref[...] = limits(fresh_table_ref, fresh_offset_ref)
    copies[0].wait()
    copies[1].wait()
    part_ref[Q:] = jnp.full((TAIL, WIDE), -1e30, F32)
    for g in range(KV):
        best = masked_scores(g, q_ref[...], pack_ref[:KEYS, g * HD : (g + 1) * HD], bounds, s_ref)
        part_ref[Q + g : Q + g + 1, :ROWS] = best
    load.wait()
    store = pltpu.make_async_copy(pack_ref, pack_hbm, sems.at[4 + count])
    store.start()
    copies[2].wait()
    grad = split(g_ref[...])
    for i in range(count):
        copies[3 + i].wait()
        part = slice(i * tile, (i + 1) * tile)
        part_ref[:Q, part] = dot3(grad, split(w_ref[part]), NT)
    store.wait()


def front(queries, keys, values, grad, w_out, table, offset, fresh_table, fresh_offset):
    hbm, smem, vmem = (pl.BlockSpec(memory_space=m) for m in (pltpu.HBM, pltpu.SMEM, pltpu.VMEM))
    outs = [SCORES, WITH_ROWS, PACK, ((TAIL, KV * HD), F32)]
    return pl.pallas_call(
        front_body,
        out_shape=[jax.ShapeDtypeStruct(s, d) for s, d in outs],
        in_specs=[hbm] * 5 + [smem] * 4,
        out_specs=[vmem, vmem, hbm, vmem],
        scratch_shapes=[
            pltpu.VMEM((Q, WIDE), F32),
            pltpu.VMEM(PACK[0], F32),
            pltpu.VMEM((Q, WIDE), F32),
            pltpu.VMEM((WIDE, WIDE), F32),
            pltpu.SemaphoreType.DMA((8,)),
        ],
        cost_estimate=pl.CostEstimate(flops=0, bytes_accessed=0, transcendentals=0),
        compiler_params=pltpu.CompilerParams(vmem_limit_bytes=FRONT_MB << 20),
    )(queries, keys, values, grad, w_out, table, offset, fresh_table, fresh_offset)


def joined(mine, other):
    first = lax.axis_index("head") % 2 == 0
    return jnp.concatenate([jnp.where(first, mine, other), jnp.where(first, other, mine)], 0)


def dout_body(mine_ref, other_ref, fresh_ref, stats_ref, high_ref, low_ref, *refs):
    part_ref, g_ref = refs[-2:]
    final = lax.axis_index("section") == lax.axis_size("section") - 1
    g = jnp.where(final, fresh_ref[...], joined(mine_ref[...], other_ref[...]))
    g_ref[...] = g
    part_ref[:Q] = dot3(split(g), (high_ref[...], low_ref[...]), NT)
    part_ref[Q:] = stats_ref[...]


def dout_second(received, fresh, stats, high, low, *after):
    free = range(6, 6 + len(after))
    return call(dout_body, [WITH_ROWS, FULL], *received, fresh, stats, high, low, *after, free=free)


def split_body(w_ref, *refs):
    high_ref, low_ref = refs[-2:]
    high_ref[...], low_ref[...] = split(w_ref[...])


def split_weights(w, *after):
    return call(split_body, [WEIGHT, WEIGHT], w, *after, free=range(1, 1 + len(after)))


def caches_body(k_ref, v_ref, *refs):
    kt_high, kt_low, v_high, v_low = refs[-4:]
    for g in range(KV):
        kt_high[g], kt_low[g] = split(jnp.transpose(k_ref[:, g * HD : (g + 1) * HD]))
    v_high[...], v_low[...] = split(v_ref[...])


def caches(k, v, *after):
    outs = [KEYS_T, KEYS_T, CACHE_BF, CACHE_BF]
    return call(caches_body, outs, k, v, *after, free=range(2, 2 + len(after)))


def second_body(q_ref, pack_ref, k_ref, v_ref, bounds_ref, grad_ref, *refs):
    s_ref, top_ref, kt_high, kt_low, v_high, v_low, copy_ref = refs[-7:]
    final = lax.axis_index("section") == lax.axis_size("section") - 1
    bounds = jnp.where(final, bounds_ref[...], pack_ref[2 * KEYS :])
    top_ref[...] = jnp.full(top_ref.shape, -1e30, F32)
    for g in range(KV):
        cols = slice(g * HD, (g + 1) * HD)
        k = jnp.where(final, k_ref[:, cols], pack_ref[:KEYS, cols])
        top_ref[g : g + 1, :ROWS] = masked_scores(g, q_ref[0, 1], k, bounds, s_ref)
        kt_high[g], kt_low[g] = split(jnp.transpose(k))
    v_high[...], v_low[...] = split(jnp.where(final, v_ref[...], pack_ref[KEYS : 2 * KEYS]))
    copy_ref[...] = grad_ref[...]


def second(queries, pack, k_fresh, v_fresh, bounds, grad, *after):
    outs = [SCORES, STATS, KEYS_T, KEYS_T, CACHE_BF, CACHE_BF, FULL]
    free = range(6, 6 + len(after))
    return call(second_body, outs, queries, pack, k_fresh, v_fresh, bounds, grad, *after, free=free)


def products_body(d0_ref, d1_ref, s_ref, kt_high, kt_low, v_high, v_low, *refs):
    e_ref, dp_ref, a_ref, b_ref, dout_ref = refs[-5:]
    d0, d1 = d0_ref[...], d1_ref[...]
    best = jnp.maximum(d0[Q:], d1[Q:])
    dout = d0[:Q] + d1[:Q]
    dout_ref[...] = dout
    a_ref[Q:] = jnp.zeros((TAIL, WIDE), F32)
    a_groups, b_groups = [], []
    for g in range(KV):
        cols = slice(g * HD, (g + 1) * HD)
        kt = kt_high[g], kt_low[g]
        e = jnp.exp(s_ref[g] - best[g : g + 1, :ROWS])
        e_ref[g] = e
        dp = dot3((v_high[:, cols], v_low[:, cols]), split(stacked(dout, g)), NT)
        dp_ref[g] = dp
        total = jnp.sum(e, axis=0, keepdims=True)
        delta = jnp.sum(e * dp, axis=0, keepdims=True)
        mean = jnp.where(total > 0, delta / total, 0.0)
        b = jnp.transpose(dot3(kt, split(e), NN))
        centred = jnp.transpose(dot3(kt, split(e * (dp - mean)), NN))
        a_groups.append(centred + as_columns(mean) * b)
        b_groups.append(b)
        a_ref[Q + g : Q + g + 1, :ROWS] = delta
        a_ref[Q + KV + g : Q + KV + g + 1, :ROWS] = total
    a_ref[:Q] = spread(a_groups)
    b_ref[...] = spread(b_groups)


def products(dout, s, kt_high, kt_low, v_high, v_low, *after):
    outs = [SCORES, SCORES, WITH_ROWS, FULL, FULL]
    free = range(7, 7 + len(after))
    return call(products_body, outs, *dout, s, kt_high, kt_low, v_high, v_low, *after, free=free)


def input_body(step, a0, a1, b0, b1, g_ref, high_ref, low_ref, *refs):
    head = lax.axis_index("head")
    a_all, b_all = a0[...] + a1[...], b0[...] + b1[...]
    refs[-1][...] = a_all[Q:]
    groups = []
    for g in range(KV):
        total = a_all[Q + KV + g : Q + KV + g + 1, :ROWS]
        delta = a_all[Q + g : Q + g + 1, :ROWS] / total
        a, b = stacked(a_all[:Q], g), stacked(b_all, g)
        groups.append((a - as_columns(delta) * b) * as_columns(SCALE / total))
    part = dot3(split(spread(groups)), (high_ref[...], low_ref[...]), NT)
    part = part + jnp.where(head == 0, g_ref[...], 0.0)
    if step == 1:
        refs[-2][...] = part
        return
    keep_ref, send_ref = refs[-3:-1]
    first = head % 2 == 0
    keep_ref[...] = jnp.where(first, part[:HALF], part[HALF:])
    send_ref[...] = jnp.where(first, part[HALF:], part[:HALF])


def input_gradient(step, a, b, g, high, low, *after):
    outs = [PIECE, PIECE, STATS] if step == 0 else [FULL, STATS]
    return call(functools.partial(input_body, step), outs, *a, *b, g, high, low, *after, free=range(7, 7 + len(after)))


def sums_body(step, row_ref, e_ref, dp_ref, dout_ref, q_ref, *refs):
    if step == 0:
        key_in, value_in, both_out = refs[0].at[0], refs[1].at[0], refs[-1]
        key_out, value_out = both_out.at[:KEYS], both_out.at[KEYS:]
    else:
        key_in, value_in = refs[0].at[:KEYS], refs[0].at[KEYS:]
        key_out, value_out = refs[-2:]
    for g in range(KV):
        total = row_ref[KV + g : KV + g + 1, :ROWS]
        delta = row_ref[g : g + 1, :ROWS] / total
        probs = e_ref[g] * (1.0 / total)
        d_score = probs * (dp_ref[g] - delta)
        cols = slice(g * HD, (g + 1) * HD)
        value_out[:, cols] = value_in[:, cols] + dot3(split(probs), split(stacked(dout_ref[...], g)), NN)
        q = split(stacked(q_ref[0, step], g))
        key_out[:, cols] = key_in[:, cols] + SCALE * dot3(split(d_score), q, NN)


def gradient_sums(step, rows, e, dp, dout, queries, sums, *after):
    outs = [((2 * KEYS, KV * HD), F32)] if step == 0 else [CACHE, CACHE]
    count = 5 + len(sums)
    free = range(count, count + len(after))
    return call(functools.partial(sums_body, step), outs, rows, e, dp, dout, queries, *sums, *after, free=free)


def swap(bits, n=4):
    return [(i, i ^ bits) for i in range(n)]


def neighbours(turn):
    return [(h * 4 + p, h * 4 + (p ^ (1 if (h + turn) % 2 == 0 else 3))) for h in range(4) for p in range(4)]


def page_sum(x, join=jnp.add):
    x = join(x, lax.ppermute(x, ("head", "page"), neighbours(0)))
    return x, lax.ppermute(x, ("head", "page"), neighbours(1))


def sum_and_top(a, b):
    rows = lax.broadcasted_iota(jnp.int32, a.shape, 0)
    return jnp.where(rows < Q, a + b, jnp.maximum(a, b))


def tied(value, after):
    return lax.optimization_barrier((value, after))[0]


def per_device(
    grad_in, grad_fresh, queries, key_cache, value_cache, key_fresh, value_fresh, key_grad_in, value_grad_in,
    page_table, offsets, page_fresh, offset_fresh, w_query, w_out,
):
    back_section = [(i, i - 1) for i in range(1, 16)]

    s1, part, pack, fresh_bounds = front(
        queries, key_cache, value_cache, grad_in, w_out, page_table[0], offsets, page_fresh, offset_fresh
    )
    dout1 = page_sum(part, sum_and_top)
    pack2 = lax.ppermute(pack, "section", back_section)
    split1 = caches(key_cache[0], value_cache[0], dout1[0])
    wq_high, wq_low = split_weights(w_query[0], dout1[0])
    e1, dp1, a, b, dout1 = products(dout1, s1, *split1, wq_high)
    a1, b1 = page_sum(a), page_sum(b)
    wo_high, wo_low = split_weights(w_out[0], a1[0])
    keep, send, rows1 = input_gradient(0, a1, b1, grad_in[0], wq_high, wq_low, wo_high)
    part = keep + lax.ppermute(send, "head", swap(1))
    (sums,) = gradient_sums(0, rows1, e1, dp1, dout1, queries, (key_grad_in, value_grad_in), part)
    part = part + lax.ppermute(part, "head", swap(2))
    mine = lax.ppermute(tied(part, sums), "section", back_section)
    s2, m2, *split2, fresh = second(queries, pack2, key_fresh, value_fresh, fresh_bounds, grad_fresh, part)
    mine = tied(mine, m2)
    other = lax.ppermute(mine, "head", swap(1))

    part, g2 = dout_second((mine, other), fresh, m2, wo_high, wo_low, sums)
    dout2 = page_sum(part, sum_and_top)
    sums = lax.ppermute(tied(sums, part), "section", back_section)
    e2, dp2, a, b, dout2 = products(dout2, s2, *split2)
    a2, b2 = page_sum(a), page_sum(b)
    part, rows2 = input_gradient(1, a2, b2, g2, wq_high, wq_low)
    part = part + lax.ppermute(part, "head", swap(1))
    key_final, value_final = gradient_sums(1, rows2, e2, dp2, dout2, queries, (sums,), part)
    grad_done = part + tied(lax.ppermute(part, "head", swap(2)), key_final)
    return (grad_done[None], key_final[None], value_final[None])


def solution(mesh):
    placed = (
        P("section", None, "page"),
        P(None, "page"),
        P("section", None, None, "head"),
        P("section", "page", "head"),
        P("section", "page", "head"),
        P("page", "head"),
        P("page", "head"),
        P("section", "page", "head"),
        P("section", "page", "head"),
        P("section", None),
        P("section"),
        P(),
        P(),
        P("section", "page", "head"),
        P("section", "head", "page"),
    )
    return jax.shard_map(
        per_device,
        mesh=mesh,
        in_specs=placed,
        out_specs=(
            P("section", None, "page"),
            P("section", "page", "head"),
            P("section", "page", "head"),
        ),
        check_vma=False,
    )
```

```python
import functools

import jax
import jax.numpy as jnp
from jax import lax
from jax.experimental import pallas as pl
from jax.experimental.pallas import tpu as pltpu
from jax.sharding import PartitionSpec as P

HD = 128
BLOCK = 128
Q = 64
HALF = Q // 2
FRONT_MB = 60
TAIL = 8
KEYS = 512
KV = 2
GROUP = 3
ROWS = GROUP * Q
WIDE = KV * GROUP * HD
SCALE = HD ** (-0.5)
F32 = jnp.float32
BF16 = jnp.bfloat16
NN = (((1,), (0,)), ((), ()))
NT = (((1,), (1,)), ((), ()))


def split(x):
    high = x.astype(BF16)
    return high, (x - high.astype(F32)).astype(BF16)


def dot(a, b, dims):
    return lax.dot_general(a, b, dims, preferred_element_type=F32)


def dot3(a, b, dims):
    (a_high, a_low), (b_high, b_low) = a, b
    return dot(a_high, b_high, dims) + (dot(a_low, b_high, dims) + dot(a_high, b_low, dims))


def dot3_few(a, b, dims):
    (a_high, a_low), (b_high, b_low) = a, b
    rows = a_high.shape[0]
    both = dot(jnp.concatenate([a_high, a_low], 0), b_high, dims)
    return both[:rows] + (both[rows:] + dot(a_high, b_low, dims))


def key_sum(kt, x):
    high, low = split(x)
    both = dot(kt, high, NN)
    return both[:HD] + (both[HD:] + dot(kt[:HD], low, NN))


def stacked(x, g):
    return jnp.concatenate([x[:, (g * GROUP + r) * HD : (g * GROUP + r + 1) * HD] for r in range(GROUP)], 0)


def spread(groups):
    return jnp.concatenate([groups[g][r * Q : (r + 1) * Q] for g in range(KV) for r in range(GROUP)], 1)


def as_columns(row):
    return jnp.transpose(jnp.broadcast_to(row, (HD, ROWS)))


def call(body, outs, *args, scratch=(), mb=6, smem=(), free=()):
    spaces = [pltpu.SMEM if i in smem else pl.ANY if i in free else pltpu.VMEM for i in range(len(args))]
    return pl.pallas_call(
        body,
        out_shape=[jax.ShapeDtypeStruct(s, d) for s, d in outs],
        in_specs=[pl.BlockSpec(memory_space=space) for space in spaces],
        out_specs=[pl.BlockSpec(memory_space=pltpu.VMEM)] * len(outs),
        scratch_shapes=scratch,
        cost_estimate=pl.CostEstimate(flops=0, bytes_accessed=0, transcendentals=0),
        compiler_params=pltpu.CompilerParams(vmem_limit_bytes=mb << 20),
    )(*args)


SCORES = ((KV, KEYS, ROWS), F32)
CACHE = ((KEYS, KV * HD), F32)
FULL = ((Q, WIDE), F32)
PIECE = ((HALF, WIDE), F32)
WITH_ROWS = ((Q + TAIL, WIDE), F32)
STATS = ((TAIL, WIDE), F32)
PACK = ((2 * KEYS + TAIL, KV * HD), F32)
WEIGHT = ((WIDE, WIDE), BF16)
KEYS_T = ((KV, 2 * HD, KEYS), BF16)
VALUES = ((KEYS, 2 * KV * HD), BF16)


def limits(table_ref, offset_ref):
    page = lax.axis_index("page")
    rows = []
    for b in range(8):
        bound = offset_ref[0] - table_ref[page * 4 + b % 4] * BLOCK
        rows.append(jnp.full((1, KV * HD), bound, jnp.int32).astype(F32))
    return jnp.concatenate(rows, 0)


def masked_scores(g, q, k, bounds, s_ref):
    lead = (
        lax.broadcasted_iota(jnp.int32, (BLOCK, ROWS), 0) - lax.broadcasted_iota(jnp.int32, (BLOCK, ROWS), 1) % Q
    ).astype(F32)
    s = lax.dot_general(
        k, stacked(q, g), NT, precision=lax.Precision.HIGHEST, preferred_element_type=F32
    ) * SCALE
    best = None
    for b in range(KEYS // BLOCK):
        block = jnp.where(lead <= bounds[b : b + 1, :ROWS], s[b * BLOCK : (b + 1) * BLOCK], -1e30)
        s_ref[g, b * BLOCK : (b + 1) * BLOCK] = block
        most = jnp.max(block, axis=0, keepdims=True)
        best = most if best is None else jnp.maximum(best, most)
    return best


def front_body(
    q_hbm, k_hbm, v_hbm, g_hbm, w_hbm, table_ref, offset_ref, fresh_table_ref, fresh_offset_ref,
    s_ref, part_ref, pack_hbm, fresh_ref,
    q_ref, pack_ref, g_ref, w_ref, sems,
):
    count = 3
    tile = WIDE // count
    copies = [
        pltpu.make_async_copy(q_hbm.at[0, 0], q_ref, sems.at[0]),
        pltpu.make_async_copy(k_hbm.at[0], pack_ref.at[pl.ds(0, KEYS)], sems.at[1]),
        pltpu.make_async_copy(g_hbm.at[0], g_ref, sems.at[2]),
    ]
    for i in range(2 * count):
        part = pl.ds(i * tile // 2, tile // 2)
        copies.append(pltpu.make_async_copy(w_hbm.at[0, part], w_ref.at[part], sems.at[3 + i]))
    for copy in copies:
        copy.start()
    load = pltpu.make_async_copy(v_hbm.at[0], pack_ref.at[pl.ds(KEYS, KEYS)], sems.at[3 + 2 * count])
    load.start()
    bounds = limits(table_ref, offset_ref)
    pack_ref[2 * KEYS :] = bounds
    fresh_ref[...] = limits(fresh_table_ref, fresh_offset_ref)
    copies[0].wait()
    copies[1].wait()
    part_ref[Q:] = jnp.full((TAIL, WIDE), -1e30, F32)
    for g in range(KV):
        best = masked_scores(g, q_ref[...], pack_ref[:KEYS, g * HD : (g + 1) * HD], bounds, s_ref)
        part_ref[Q + g : Q + g + 1, :ROWS] = best
    load.wait()
    store = pltpu.make_async_copy(pack_ref, pack_hbm, sems.at[4 + 2 * count])
    store.start()
    copies[2].wait()
    grad = split(g_ref[...])
    for i in range(count):
        copies[3 + 2 * i].wait()
        copies[4 + 2 * i].wait()
        part = slice(i * tile, (i + 1) * tile)
        part_ref[:Q, part] = dot3_few(grad, split(w_ref[part]), NT)
    store.wait()


def front(queries, keys, values, grad, w_out, table, offset, fresh_table, fresh_offset):
    hbm, smem, vmem = (pl.BlockSpec(memory_space=m) for m in (pltpu.HBM, pltpu.SMEM, pltpu.VMEM))
    outs = [SCORES, WITH_ROWS, PACK, ((TAIL, KV * HD), F32)]
    return pl.pallas_call(
        front_body,
        out_shape=[jax.ShapeDtypeStruct(s, d) for s, d in outs],
        in_specs=[hbm] * 5 + [smem] * 4,
        out_specs=[vmem, vmem, hbm, vmem],
        scratch_shapes=[
            pltpu.VMEM((Q, WIDE), F32),
            pltpu.VMEM(PACK[0], F32),
            pltpu.VMEM((Q, WIDE), F32),
            pltpu.VMEM((WIDE, WIDE), F32),
            pltpu.SemaphoreType.DMA((11,)),
        ],
        cost_estimate=pl.CostEstimate(flops=0, bytes_accessed=0, transcendentals=0),
        compiler_params=pltpu.CompilerParams(vmem_limit_bytes=FRONT_MB << 20),
    )(queries, keys, values, grad, w_out, table, offset, fresh_table, fresh_offset)


def joined(mine, other):
    first = lax.axis_index("head") % 2 == 0
    return jnp.concatenate([jnp.where(first, mine, other), jnp.where(first, other, mine)], 0)


def dout_body(mine_ref, other_ref, fresh_ref, stats_ref, high_ref, low_ref, *refs):
    part_ref, g_ref = refs[-2:]
    final = lax.axis_index("section") == lax.axis_size("section") - 1
    g = jnp.where(final, fresh_ref[...], joined(mine_ref[...], other_ref[...]))
    g_ref[...] = g
    part_ref[:Q] = dot3_few(split(g), (high_ref[...], low_ref[...]), NT)
    part_ref[Q:] = stats_ref[...]


def dout_second(received, fresh, stats, high, low, *after):
    free = range(6, 6 + len(after))
    return call(dout_body, [WITH_ROWS, FULL], *received, fresh, stats, high, low, *after, free=free)


def split_body(w_ref, *refs):
    high_ref, low_ref = refs[-2:]
    high_ref[...], low_ref[...] = split(w_ref[...])


def split_weights(w, *after):
    return call(split_body, [WEIGHT, WEIGHT], w, *after, free=range(1, 1 + len(after)))


def store_keys(kt_ref, g, k):
    kt_ref[g, :HD], kt_ref[g, HD:] = split(jnp.transpose(k))


def store_values(v_ref, g, v):
    v_ref[:, 2 * g * HD : (2 * g + 1) * HD], v_ref[:, (2 * g + 1) * HD : (2 * g + 2) * HD] = split(v)


def caches_body(k_ref, v_ref, *refs):
    kt_ref, v_out = refs[-2:]
    for g in range(KV):
        cols = slice(g * HD, (g + 1) * HD)
        store_keys(kt_ref, g, k_ref[:, cols])
        store_values(v_out, g, v_ref[:, cols])


def caches(k, v, *after):
    return call(caches_body, [KEYS_T, VALUES], k, v, *after, free=range(2, 2 + len(after)))


def second_body(q_ref, pack_ref, k_ref, v_ref, bounds_ref, grad_ref, *refs):
    s_ref, top_ref, kt_ref, v_out, copy_ref = refs[-5:]
    final = lax.axis_index("section") == lax.axis_size("section") - 1
    bounds = jnp.where(final, bounds_ref[...], pack_ref[2 * KEYS :])
    top_ref[...] = jnp.full(top_ref.shape, -1e30, F32)
    for g in range(KV):
        cols = slice(g * HD, (g + 1) * HD)
        k = jnp.where(final, k_ref[:, cols], pack_ref[:KEYS, cols])
        top_ref[g : g + 1, :ROWS] = masked_scores(g, q_ref[0, 1], k, bounds, s_ref)
        store_keys(kt_ref, g, k)
        store_values(v_out, g, jnp.where(final, v_ref[:, cols], pack_ref[KEYS : 2 * KEYS, cols]))
    copy_ref[...] = grad_ref[...]


def second(queries, pack, k_fresh, v_fresh, bounds, grad, *after):
    outs = [SCORES, STATS, KEYS_T, VALUES, FULL]
    free = range(6, 6 + len(after))
    return call(second_body, outs, queries, pack, k_fresh, v_fresh, bounds, grad, *after, free=free)


def products_body(d0_ref, d1_ref, s_ref, kt_ref, v_ref, *refs):
    e_ref, dp_ref, a_ref, b_ref, dout_ref = refs[-5:]
    d0, d1 = d0_ref[...], d1_ref[...]
    best = jnp.maximum(d0[Q:], d1[Q:])
    dout = d0[:Q] + d1[:Q]
    dout_ref[...] = dout
    a_ref[Q:] = jnp.zeros((TAIL, WIDE), F32)
    a_groups, b_groups = [], []
    for g in range(KV):
        e = jnp.exp(s_ref[g] - best[g : g + 1, :ROWS])
        e_ref[g] = e
        high, low = split(stacked(dout, g))
        v = v_ref[:, 2 * g * HD : (2 * g + 2) * HD]
        dp = dot(v, jnp.concatenate([high, high], 1), NT) + dot(v[:, :HD], low, NT)
        dp_ref[g] = dp
        total = jnp.sum(e, axis=0, keepdims=True)
        delta = jnp.sum(e * dp, axis=0, keepdims=True)
        mean = jnp.where(total > 0, delta / total, 0.0)
        b = jnp.transpose(key_sum(kt_ref[g], e))
        centred = jnp.transpose(key_sum(kt_ref[g], e * (dp - mean)))
        a_groups.append(centred + as_columns(mean) * b)
        b_groups.append(b)
        a_ref[Q + g : Q + g + 1, :ROWS] = delta
        a_ref[Q + KV + g : Q + KV + g + 1, :ROWS] = total
    a_ref[:Q] = spread(a_groups)
    b_ref[...] = spread(b_groups)


def products(dout, s, kt, v, *after):
    outs = [SCORES, SCORES, WITH_ROWS, FULL, FULL]
    free = range(5, 5 + len(after))
    return call(products_body, outs, *dout, s, kt, v, *after, free=free)


def input_body(step, a0, a1, b0, b1, g_ref, high_ref, low_ref, *refs):
    head = lax.axis_index("head")
    a_all, b_all = a0[...] + a1[...], b0[...] + b1[...]
    refs[-1][...] = a_all[Q:]
    groups = []
    for g in range(KV):
        total = a_all[Q + KV + g : Q + KV + g + 1, :ROWS]
        delta = a_all[Q + g : Q + g + 1, :ROWS] / total
        a, b = stacked(a_all[:Q], g), stacked(b_all, g)
        groups.append((a - as_columns(delta) * b) * as_columns(SCALE / total))
    part = dot3_few(split(spread(groups)), (high_ref[...], low_ref[...]), NT)
    part = part + jnp.where(head == 0, g_ref[...], 0.0)
    if step == 1:
        refs[-2][...] = part
        return
    keep_ref, send_ref = refs[-3:-1]
    first = head % 2 == 0
    keep_ref[...] = jnp.where(first, part[:HALF], part[HALF:])
    send_ref[...] = jnp.where(first, part[HALF:], part[:HALF])


def input_gradient(step, a, b, g, high, low, *after):
    outs = [PIECE, PIECE, STATS] if step == 0 else [FULL, STATS]
    return call(functools.partial(input_body, step), outs, *a, *b, g, high, low, *after, free=range(7, 7 + len(after)))


def sums_body(step, row_ref, e_ref, dp_ref, dout_ref, q_ref, *refs):
    if step == 0:
        key_in, value_in, both_out = refs[0].at[0], refs[1].at[0], refs[-1]
        key_out, value_out = both_out.at[:KEYS], both_out.at[KEYS:]
    else:
        key_in, value_in = refs[0].at[:KEYS], refs[0].at[KEYS:]
        key_out, value_out = refs[-2:]
    for g in range(KV):
        total = row_ref[KV + g : KV + g + 1, :ROWS]
        delta = row_ref[g : g + 1, :ROWS] / total
        probs = e_ref[g] * (1.0 / total)
        d_score = probs * (dp_ref[g] - delta)
        cols = slice(g * HD, (g + 1) * HD)
        value_out[:, cols] = value_in[:, cols] + dot3(split(probs), split(stacked(dout_ref[...], g)), NN)
        q = split(stacked(q_ref[0, step], g))
        key_out[:, cols] = key_in[:, cols] + SCALE * dot3(split(d_score), q, NN)


def gradient_sums(step, rows, e, dp, dout, queries, sums, *after):
    outs = [((2 * KEYS, KV * HD), F32)] if step == 0 else [CACHE, CACHE]
    count = 5 + len(sums)
    free = range(count, count + len(after))
    return call(functools.partial(sums_body, step), outs, rows, e, dp, dout, queries, *sums, *after, free=free)


def swap(bits, n=4):
    return [(i, i ^ bits) for i in range(n)]


def neighbours(turn):
    return [(h * 4 + p, h * 4 + (p ^ (1 if (h + turn) % 2 == 0 else 3))) for h in range(4) for p in range(4)]


def page_sum(x, join=jnp.add):
    x = join(x, lax.ppermute(x, ("head", "page"), neighbours(0)))
    return x, lax.ppermute(x, ("head", "page"), neighbours(1))


def sum_and_top(a, b):
    rows = lax.broadcasted_iota(jnp.int32, a.shape, 0)
    return jnp.where(rows < Q, a + b, jnp.maximum(a, b))


def tied(value, after):
    return lax.optimization_barrier((value, after))[0]


def per_device(
    grad_in, grad_fresh, queries, key_cache, value_cache, key_fresh, value_fresh, key_grad_in, value_grad_in,
    page_table, offsets, page_fresh, offset_fresh, w_query, w_out,
):
    back_section = [(i, i - 1) for i in range(1, 16)]

    s1, part, pack, fresh_bounds = front(
        queries, key_cache, value_cache, grad_in, w_out, page_table[0], offsets, page_fresh, offset_fresh
    )
    dout1 = page_sum(part, sum_and_top)
    pack2 = lax.ppermute(pack, "section", back_section)
    split1 = caches(key_cache[0], value_cache[0], dout1[0])
    wq_high, wq_low = split_weights(w_query[0], dout1[0])
    e1, dp1, a, b, dout1 = products(dout1, s1, *split1, wq_high)
    a1, b1 = page_sum(a), page_sum(b)
    wo_high, wo_low = split_weights(w_out[0], a1[0])
    keep, send, rows1 = input_gradient(0, a1, b1, grad_in[0], wq_high, wq_low, wo_high)
    part = keep + lax.ppermute(send, "head", swap(1))
    (sums,) = gradient_sums(0, rows1, e1, dp1, dout1, queries, (key_grad_in, value_grad_in), part)
    part = part + lax.ppermute(part, "head", swap(2))
    mine = lax.ppermute(tied(part, sums), "section", back_section)
    s2, m2, *split2, fresh = second(queries, pack2, key_fresh, value_fresh, fresh_bounds, grad_fresh, part)
    mine = tied(mine, m2)
    other = lax.ppermute(mine, "head", swap(1))

    part, g2 = dout_second((mine, other), fresh, m2, wo_high, wo_low, sums)
    dout2 = page_sum(part, sum_and_top)
    sums = lax.ppermute(tied(sums, part), "section", back_section)
    e2, dp2, a, b, dout2 = products(dout2, s2, *split2)
    a2, b2 = page_sum(a), page_sum(b)
    part, rows2 = input_gradient(1, a2, b2, g2, wq_high, wq_low)
    part = part + lax.ppermute(part, "head", swap(1))
    key_final, value_final = gradient_sums(1, rows2, e2, dp2, dout2, queries, (sums,), part)
    grad_done = part + tied(lax.ppermute(part, "head", swap(2)), key_final)
    return (grad_done[None], key_final[None], value_final[None])


def solution(mesh):
    placed = (
        P("section", None, "page"),
        P(None, "page"),
        P("section", None, None, "head"),
        P("section", "page", "head"),
        P("section", "page", "head"),
        P("page", "head"),
        P("page", "head"),
        P("section", "page", "head"),
        P("section", "page", "head"),
        P("section", None),
        P("section"),
        P(),
        P(),
        P("section", "page", "head"),
        P("section", "head", "page"),
    )
    return jax.shard_map(
        per_device,
        mesh=mesh,
        in_specs=placed,
        out_specs=(
            P("section", None, "page"),
            P("section", "page", "head"),
            P("section", "page", "head"),
        ),
        check_vma=False,
    )
```

```python
import functools

import jax
import jax.numpy as jnp
from jax import lax
from jax.experimental import pallas as pl
from jax.experimental.pallas import tpu as pltpu
from jax.sharding import PartitionSpec as P

HD = 128
BLOCK = 128
Q = 64
HALF = Q // 2
FRONT_MB = 60
TAIL = 8
KEYS = 512
KV = 2
GROUP = 3
ROWS = GROUP * Q
WIDE = KV * GROUP * HD
SCALE = HD ** (-0.5)
F32 = jnp.float32
BF16 = jnp.bfloat16
NN = (((1,), (0,)), ((), ()))
NT = (((1,), (1,)), ((), ()))


def split(x):
    high = x.astype(BF16)
    return high, (x - high.astype(F32)).astype(BF16)


def dot(a, b, dims):
    return lax.dot_general(a, b, dims, preferred_element_type=F32)


def dot3(a, b, dims):
    (a_high, a_low), (b_high, b_low) = a, b
    return dot(a_high, b_high, dims) + (dot(a_low, b_high, dims) + dot(a_high, b_low, dims))


def dot3_few(a, b, dims):
    (a_high, a_low), (b_high, b_low) = a, b
    rows = a_high.shape[0]
    both = dot(jnp.concatenate([a_high, a_low], 0), b_high, dims)
    return both[:rows] + (both[rows:] + dot(a_high, b_low, dims))


def key_sum(kt, x):
    high, low = split(x)
    both = dot(kt, high, NN)
    return both[:HD] + (both[HD:] + dot(kt[:HD], low, NN))


def stacked(x, g):
    return jnp.concatenate([x[:, (g * GROUP + r) * HD : (g * GROUP + r + 1) * HD] for r in range(GROUP)], 0)


def spread(groups):
    return jnp.concatenate([groups[g][r * Q : (r + 1) * Q] for g in range(KV) for r in range(GROUP)], 1)


def as_columns(row):
    return jnp.transpose(jnp.broadcast_to(row, (HD, ROWS)))


def call(body, outs, *args, scratch=(), mb=6, smem=(), free=()):
    spaces = [pltpu.SMEM if i in smem else pl.ANY if i in free else pltpu.VMEM for i in range(len(args))]
    return pl.pallas_call(
        body,
        out_shape=[jax.ShapeDtypeStruct(s, d) for s, d in outs],
        in_specs=[pl.BlockSpec(memory_space=space) for space in spaces],
        out_specs=[pl.BlockSpec(memory_space=pltpu.VMEM)] * len(outs),
        scratch_shapes=scratch,
        cost_estimate=pl.CostEstimate(flops=0, bytes_accessed=0, transcendentals=0),
        compiler_params=pltpu.CompilerParams(vmem_limit_bytes=mb << 20),
    )(*args)


SCORES = ((KV, KEYS, ROWS), F32)
CACHE = ((KEYS, KV * HD), F32)
FULL = ((Q, WIDE), F32)
PIECE = ((HALF, WIDE), F32)
WITH_ROWS = ((Q + TAIL, WIDE), F32)
STATS = ((TAIL, WIDE), F32)
PACK = ((2 * KEYS + TAIL, KV * HD), F32)
WEIGHT = ((WIDE, WIDE), BF16)
KEYS_T = ((KV, 2 * HD, KEYS), BF16)
VALUES = ((KEYS, 2 * KV * HD), BF16)


def limits(table_ref, offset_ref):
    page = lax.axis_index("page")
    rows = []
    for b in range(8):
        bound = offset_ref[0] - table_ref[page * 4 + b % 4] * BLOCK
        rows.append(jnp.full((1, KV * HD), bound, jnp.int32).astype(F32))
    return jnp.concatenate(rows, 0)


def masked_scores(g, q, k, bounds, s_ref):
    lead = (
        lax.broadcasted_iota(jnp.int32, (BLOCK, ROWS), 0) - lax.broadcasted_iota(jnp.int32, (BLOCK, ROWS), 1) % Q
    ).astype(F32)
    s = lax.dot_general(
        k, stacked(q, g), NT, precision=lax.Precision.HIGHEST, preferred_element_type=F32
    ) * SCALE
    best = None
    for b in range(KEYS // BLOCK):
        block = jnp.where(lead <= bounds[b : b + 1, :ROWS], s[b * BLOCK : (b + 1) * BLOCK], -1e30)
        s_ref[g, b * BLOCK : (b + 1) * BLOCK] = block
        most = jnp.max(block, axis=0, keepdims=True)
        best = most if best is None else jnp.maximum(best, most)
    return best


def front_body(
    q_hbm, k_hbm, v_hbm, g_hbm, w_hbm, table_ref, offset_ref, fresh_table_ref, fresh_offset_ref,
    s_ref, part_ref, pack_hbm, fresh_ref,
    q_ref, pack_ref, g_ref, w_ref, sems,
):
    count = 3
    tile = WIDE // count
    copies = [
        pltpu.make_async_copy(q_hbm.at[0, 0], q_ref, sems.at[0]),
        pltpu.make_async_copy(k_hbm.at[0], pack_ref.at[pl.ds(0, KEYS)], sems.at[1]),
        pltpu.make_async_copy(g_hbm.at[0], g_ref, sems.at[2]),
    ]
    for i in range(2 * count):
        part = pl.ds(i * tile // 2, tile // 2)
        copies.append(pltpu.make_async_copy(w_hbm.at[0, part], w_ref.at[part], sems.at[3 + i]))
    for copy in copies:
        copy.start()
    load = pltpu.make_async_copy(v_hbm.at[0], pack_ref.at[pl.ds(KEYS, KEYS)], sems.at[3 + 2 * count])
    load.start()
    bounds = limits(table_ref, offset_ref)
    pack_ref[2 * KEYS :] = bounds
    fresh_ref[...] = limits(fresh_table_ref, fresh_offset_ref)
    copies[0].wait()
    copies[1].wait()
    part_ref[Q:] = jnp.full((TAIL, WIDE), -1e30, F32)
    for g in range(KV):
        best = masked_scores(g, q_ref[...], pack_ref[:KEYS, g * HD : (g + 1) * HD], bounds, s_ref)
        part_ref[Q + g : Q + g + 1, :ROWS] = best
    load.wait()
    store = pltpu.make_async_copy(pack_ref, pack_hbm, sems.at[4 + 2 * count])
    store.start()
    copies[2].wait()
    grad = split(g_ref[...])
    for i in range(count):
        copies[3 + 2 * i].wait()
        copies[4 + 2 * i].wait()
        part = slice(i * tile, (i + 1) * tile)
        part_ref[:Q, part] = dot3_few(grad, split(w_ref[part]), NT)
    store.wait()


def front(queries, keys, values, grad, w_out, table, offset, fresh_table, fresh_offset):
    hbm, smem, vmem = (pl.BlockSpec(memory_space=m) for m in (pltpu.HBM, pltpu.SMEM, pltpu.VMEM))
    outs = [SCORES, WITH_ROWS, PACK, ((TAIL, KV * HD), F32)]
    return pl.pallas_call(
        front_body,
        out_shape=[jax.ShapeDtypeStruct(s, d) for s, d in outs],
        in_specs=[hbm] * 5 + [smem] * 4,
        out_specs=[vmem, vmem, hbm, vmem],
        scratch_shapes=[
            pltpu.VMEM((Q, WIDE), F32),
            pltpu.VMEM(PACK[0], F32),
            pltpu.VMEM((Q, WIDE), F32),
            pltpu.VMEM((WIDE, WIDE), F32),
            pltpu.SemaphoreType.DMA((11,)),
        ],
        cost_estimate=pl.CostEstimate(flops=0, bytes_accessed=0, transcendentals=0),
        compiler_params=pltpu.CompilerParams(vmem_limit_bytes=FRONT_MB << 20),
    )(queries, keys, values, grad, w_out, table, offset, fresh_table, fresh_offset)


def joined(mine, other):
    first = lax.axis_index("head") % 2 == 0
    return jnp.concatenate([jnp.where(first, mine, other), jnp.where(first, other, mine)], 0)


def dout_body(mine_ref, other_ref, fresh_ref, stats_ref, high_ref, low_ref, *refs):
    part_ref, g_ref = refs[-2:]
    final = lax.axis_index("section") == lax.axis_size("section") - 1
    g = jnp.where(final, fresh_ref[...], joined(mine_ref[...], other_ref[...]))
    g_ref[...] = g
    part_ref[:Q] = dot3_few(split(g), (high_ref[...], low_ref[...]), NT)
    part_ref[Q:] = stats_ref[...]


def dout_second(received, fresh, stats, high, low, *after):
    free = range(6, 6 + len(after))
    return call(dout_body, [WITH_ROWS, FULL], *received, fresh, stats, high, low, *after, free=free)


def split_body(w_ref, *refs):
    high_ref, low_ref = refs[-2:]
    high_ref[...], low_ref[...] = split(w_ref[...])


def split_weights(w, *after):
    return call(split_body, [WEIGHT, WEIGHT], w, *after, free=range(1, 1 + len(after)))


def store_keys(kt_ref, g, k):
    kt_ref[g, :HD], kt_ref[g, HD:] = split(jnp.transpose(k))


def store_values(v_ref, g, v):
    v_ref[:, 2 * g * HD : (2 * g + 1) * HD], v_ref[:, (2 * g + 1) * HD : (2 * g + 2) * HD] = split(v)


def caches_body(k_ref, v_ref, part_ref, kt_ref, v_out, part_out):
    part_out[...] = part_ref[...]
    for g in range(KV):
        cols = slice(g * HD, (g + 1) * HD)
        store_keys(kt_ref, g, k_ref[:, cols])
        store_values(v_out, g, v_ref[:, cols])


def caches(k, v, part):
    return call(caches_body, [KEYS_T, VALUES, WITH_ROWS], k, v, part)


def second_body(q_ref, pack_ref, k_ref, v_ref, bounds_ref, grad_ref, *refs):
    s_ref, top_ref, kt_ref, v_out, copy_ref = refs[-5:]
    final = lax.axis_index("section") == lax.axis_size("section") - 1
    bounds = jnp.where(final, bounds_ref[...], pack_ref[2 * KEYS :])
    top_ref[...] = jnp.full(top_ref.shape, -1e30, F32)
    for g in range(KV):
        cols = slice(g * HD, (g + 1) * HD)
        k = jnp.where(final, k_ref[:, cols], pack_ref[:KEYS, cols])
        top_ref[g : g + 1, :ROWS] = masked_scores(g, q_ref[0, 1], k, bounds, s_ref)
        store_keys(kt_ref, g, k)
        store_values(v_out, g, jnp.where(final, v_ref[:, cols], pack_ref[KEYS : 2 * KEYS, cols]))
    copy_ref[...] = grad_ref[...]


def second(queries, pack, k_fresh, v_fresh, bounds, grad, *after):
    outs = [SCORES, STATS, KEYS_T, VALUES, FULL]
    free = range(6, 6 + len(after))
    return call(second_body, outs, queries, pack, k_fresh, v_fresh, bounds, grad, *after, free=free)


def products_body(d0_ref, d1_ref, s_ref, kt_ref, v_ref, *refs):
    e_ref, dp_ref, a_ref, b_ref, dout_ref = refs[-5:]
    d0, d1 = d0_ref[...], d1_ref[...]
    best = jnp.maximum(d0[Q:], d1[Q:])
    dout = d0[:Q] + d1[:Q]
    dout_ref[...] = dout
    a_ref[Q:] = jnp.zeros((TAIL, WIDE), F32)
    a_groups, b_groups = [], []
    for g in range(KV):
        e = jnp.exp(s_ref[g] - best[g : g + 1, :ROWS])
        e_ref[g] = e
        high, low = split(stacked(dout, g))
        v = v_ref[:, 2 * g * HD : (2 * g + 2) * HD]
        dp = dot(v, jnp.concatenate([high, high], 1), NT) + dot(v[:, :HD], low, NT)
        dp_ref[g] = dp
        total = jnp.sum(e, axis=0, keepdims=True)
        delta = jnp.sum(e * dp, axis=0, keepdims=True)
        mean = jnp.where(total > 0, delta / total, 0.0)
        b = jnp.transpose(key_sum(kt_ref[g], e))
        centred = jnp.transpose(key_sum(kt_ref[g], e * (dp - mean)))
        a_groups.append(centred + as_columns(mean) * b)
        b_groups.append(b)
        a_ref[Q + g : Q + g + 1, :ROWS] = delta
        a_ref[Q + KV + g : Q + KV + g + 1, :ROWS] = total
    a_ref[:Q] = spread(a_groups)
    b_ref[...] = spread(b_groups)


def products(dout, s, kt, v, *after):
    outs = [SCORES, SCORES, WITH_ROWS, FULL, FULL]
    free = range(5, 5 + len(after))
    return call(products_body, outs, *dout, s, kt, v, *after, free=free)


def input_body(step, a0, a1, b0, b1, g_ref, high_ref, low_ref, *refs):
    head = lax.axis_index("head")
    a_all, b_all = a0[...] + a1[...], b0[...] + b1[...]
    refs[-1][...] = a_all[Q:]
    groups = []
    for g in range(KV):
        total = a_all[Q + KV + g : Q + KV + g + 1, :ROWS]
        delta = a_all[Q + g : Q + g + 1, :ROWS] / total
        a, b = stacked(a_all[:Q], g), stacked(b_all, g)
        groups.append((a - as_columns(delta) * b) * as_columns(SCALE / total))
    part = dot3_few(split(spread(groups)), (high_ref[...], low_ref[...]), NT)
    part = part + jnp.where(head == 0, g_ref[...], 0.0)
    if step == 1:
        refs[-2][...] = part
        return
    keep_ref, send_ref = refs[-3:-1]
    first = head % 2 == 0
    keep_ref[...] = jnp.where(first, part[:HALF], part[HALF:])
    send_ref[...] = jnp.where(first, part[HALF:], part[:HALF])


def input_gradient(step, a, b, g, high, low, *after):
    outs = [PIECE, PIECE, STATS] if step == 0 else [FULL, STATS]
    return call(functools.partial(input_body, step), outs, *a, *b, g, high, low, *after, free=range(7, 7 + len(after)))


def sums_body(step, row_ref, e_ref, dp_ref, dout_ref, q_ref, *refs):
    if step == 0:
        key_in, value_in, both_out = refs[0].at[0], refs[1].at[0], refs[-1]
        key_out, value_out = both_out.at[:KEYS], both_out.at[KEYS:]
    else:
        key_in, value_in = refs[0].at[:KEYS], refs[0].at[KEYS:]
        key_out, value_out = refs[-2:]
    for g in range(KV):
        total = row_ref[KV + g : KV + g + 1, :ROWS]
        delta = row_ref[g : g + 1, :ROWS] / total
        probs = e_ref[g] * (1.0 / total)
        d_score = probs * (dp_ref[g] - delta)
        cols = slice(g * HD, (g + 1) * HD)
        value_out[:, cols] = value_in[:, cols] + dot3(split(probs), split(stacked(dout_ref[...], g)), NN)
        q = split(stacked(q_ref[0, step], g))
        key_out[:, cols] = key_in[:, cols] + SCALE * dot3(split(d_score), q, NN)


def gradient_sums(step, rows, e, dp, dout, queries, sums, *after):
    outs = [((2 * KEYS, KV * HD), F32)] if step == 0 else [CACHE, CACHE]
    count = 5 + len(sums)
    free = range(count, count + len(after))
    return call(functools.partial(sums_body, step), outs, rows, e, dp, dout, queries, *sums, *after, free=free)


def swap(bits, n=4):
    return [(i, i ^ bits) for i in range(n)]


def neighbours(turn):
    return [(h * 4 + p, h * 4 + (p ^ (1 if (h + turn) % 2 == 0 else 3))) for h in range(4) for p in range(4)]


def page_sum(x, join=jnp.add, held=None):
    x = join(x if held is None else held, lax.ppermute(x, ("head", "page"), neighbours(0)))
    return x, lax.ppermute(x, ("head", "page"), neighbours(1))


def sum_and_top(a, b):
    rows = lax.broadcasted_iota(jnp.int32, a.shape, 0)
    return jnp.where(rows < Q, a + b, jnp.maximum(a, b))


def tied(value, after):
    return lax.optimization_barrier((value, after))[0]


def per_device(
    grad_in, grad_fresh, queries, key_cache, value_cache, key_fresh, value_fresh, key_grad_in, value_grad_in,
    page_table, offsets, page_fresh, offset_fresh, w_query, w_out,
):
    back_section = [(i, i - 1) for i in range(1, 16)]

    s1, part, pack, fresh_bounds = front(
        queries, key_cache, value_cache, grad_in, w_out, page_table[0], offsets, page_fresh, offset_fresh
    )
    *split1, near = caches(key_cache[0], value_cache[0], part)
    dout1 = page_sum(part, sum_and_top, near)
    wq_high, wq_low = split_weights(w_query[0], dout1[0])
    pack2 = lax.ppermute(pack, "section", back_section)
    e1, dp1, a, b, dout1 = products(dout1, s1, *split1, wq_high)
    a1, b1 = page_sum(a), page_sum(b)
    wo_high, wo_low = split_weights(w_out[0], a1[0])
    keep, send, rows1 = input_gradient(0, a1, b1, grad_in[0], wq_high, wq_low, wo_high)
    part = keep + lax.ppermute(send, "head", swap(1))
    (sums,) = gradient_sums(0, rows1, e1, dp1, dout1, queries, (key_grad_in, value_grad_in), part)
    part = part + lax.ppermute(part, "head", swap(2))
    mine = lax.ppermute(tied(part, sums), "section", back_section)
    s2, m2, *split2, fresh = second(queries, pack2, key_fresh, value_fresh, fresh_bounds, grad_fresh, part)
    mine = tied(mine, m2)
    other = lax.ppermute(mine, "head", swap(1))

    part, g2 = dout_second((mine, other), fresh, m2, wo_high, wo_low, sums)
    dout2 = page_sum(part, sum_and_top)
    sums = lax.ppermute(tied(sums, m2), "section", back_section)
    e2, dp2, a, b, dout2 = products(dout2, s2, *split2)
    a2, b2 = page_sum(a), page_sum(b, lambda x, y: tied(x + y, sums))
    part, rows2 = input_gradient(1, a2, b2, g2, wq_high, wq_low)
    part = part + lax.ppermute(part, "head", swap(1))
    key_final, value_final = gradient_sums(1, rows2, e2, dp2, dout2, queries, (sums,), part)
    grad_done = part + tied(lax.ppermute(part, "head", swap(2)), key_final)
    return (grad_done[None], key_final[None], value_final[None])


def solution(mesh):
    placed = (
        P("section", None, "page"),
        P(None, "page"),
        P("section", None, None, "head"),
        P("section", "page", "head"),
        P("section", "page", "head"),
        P("page", "head"),
        P("page", "head"),
        P("section", "page", "head"),
        P("section", "page", "head"),
        P("section", None),
        P("section"),
        P(),
        P(),
        P("section", "page", "head"),
        P("section", "head", "page"),
    )
    return jax.shard_map(
        per_device,
        mesh=mesh,
        in_specs=placed,
        out_specs=(
            P("section", None, "page"),
            P("section", "page", "head"),
            P("section", "page", "head"),
        ),
        check_vma=False,
    )
```

```python
import functools

import jax
import jax.numpy as jnp
from jax import lax
from jax.experimental import pallas as pl
from jax.experimental.pallas import tpu as pltpu
from jax.sharding import PartitionSpec as P

HD = 128
BLOCK = 128
Q = 64
HALF = Q // 2
FRONT_MB = 60
TAIL = 8
KEYS = 512
KV = 2
GROUP = 3
ROWS = GROUP * Q
WIDE = KV * GROUP * HD
SCALE = HD ** (-0.5)
F32 = jnp.float32
BF16 = jnp.bfloat16
NN = (((1,), (0,)), ((), ()))
NT = (((1,), (1,)), ((), ()))


def split(x):
    high = x.astype(BF16)
    return high, (x - high.astype(F32)).astype(BF16)


def dot(a, b, dims):
    return lax.dot_general(a, b, dims, preferred_element_type=F32)


def dot3(a, b, dims):
    (a_high, a_low), (b_high, b_low) = a, b
    return dot(a_high, b_high, dims) + (dot(a_low, b_high, dims) + dot(a_high, b_low, dims))


def dot3_few(a, b, dims):
    (a_high, a_low), (b_high, b_low) = a, b
    rows = a_high.shape[0]
    both = dot(jnp.concatenate([a_high, a_low], 0), b_high, dims)
    return both[:rows] + (both[rows:] + dot(a_high, b_low, dims))


def key_sum(kt, x):
    high, low = split(x)
    both = dot(kt, high, NN)
    return both[:HD] + (both[HD:] + dot(kt[:HD], low, NN))


def stacked(x, g):
    return jnp.concatenate([x[:, (g * GROUP + r) * HD : (g * GROUP + r + 1) * HD] for r in range(GROUP)], 0)


def spread(groups):
    return jnp.concatenate([groups[g][r * Q : (r + 1) * Q] for g in range(KV) for r in range(GROUP)], 1)


def as_columns(row):
    return jnp.transpose(jnp.broadcast_to(row, (HD, ROWS)))


def call(body, outs, *args, scratch=(), mb=6, smem=(), free=()):
    spaces = [pltpu.SMEM if i in smem else pl.ANY if i in free else pltpu.VMEM for i in range(len(args))]
    return pl.pallas_call(
        body,
        out_shape=[jax.ShapeDtypeStruct(s, d) for s, d in outs],
        in_specs=[pl.BlockSpec(memory_space=space) for space in spaces],
        out_specs=[pl.BlockSpec(memory_space=pltpu.VMEM)] * len(outs),
        scratch_shapes=scratch,
        cost_estimate=pl.CostEstimate(flops=0, bytes_accessed=0, transcendentals=0),
        compiler_params=pltpu.CompilerParams(vmem_limit_bytes=mb << 20),
    )(*args)


SCORES = ((KV, KEYS, ROWS), F32)
CACHE = ((KEYS, KV * HD), F32)
FULL = ((Q, WIDE), F32)
PIECE = ((HALF, WIDE), F32)
WITH_ROWS = ((Q + TAIL, WIDE), F32)
STATS = ((TAIL, WIDE), F32)
PACK = ((2 * KEYS + TAIL, KV * HD), F32)
WEIGHT = ((WIDE, WIDE), BF16)
KEYS_T = ((KV, 2 * HD, KEYS), BF16)
VALUES = ((KEYS, 2 * KV * HD), BF16)


def limits(table_ref, offset_ref):
    page = lax.axis_index("page")
    rows = []
    for b in range(8):
        bound = offset_ref[0] - table_ref[page * 4 + b % 4] * BLOCK
        rows.append(jnp.full((1, KV * HD), bound, jnp.int32).astype(F32))
    return jnp.concatenate(rows, 0)


def masked_scores(g, q, k, bounds, s_ref):
    lead = (
        lax.broadcasted_iota(jnp.int32, (BLOCK, ROWS), 0) - lax.broadcasted_iota(jnp.int32, (BLOCK, ROWS), 1) % Q
    ).astype(F32)
    s = lax.dot_general(
        k, stacked(q, g), NT, precision=lax.Precision.HIGHEST, preferred_element_type=F32
    ) * SCALE
    best = None
    for b in range(KEYS // BLOCK):
        block = jnp.where(lead <= bounds[b : b + 1, :ROWS], s[b * BLOCK : (b + 1) * BLOCK], -1e30)
        s_ref[g, b * BLOCK : (b + 1) * BLOCK] = block
        most = jnp.max(block, axis=0, keepdims=True)
        best = most if best is None else jnp.maximum(best, most)
    return best


def front_body(
    q_hbm, k_hbm, v_hbm, g_hbm, w_hbm, table_ref, offset_ref, fresh_table_ref, fresh_offset_ref,
    s_ref, part_ref, pack_hbm, fresh_ref,
    q_ref, pack_ref, g_ref, w_ref, sems,
):
    count = 3
    tile = WIDE // count
    copies = [
        pltpu.make_async_copy(q_hbm.at[0, 0], q_ref, sems.at[0]),
        pltpu.make_async_copy(k_hbm.at[0], pack_ref.at[pl.ds(0, KEYS)], sems.at[1]),
        pltpu.make_async_copy(g_hbm.at[0], g_ref, sems.at[2]),
    ]
    for i in range(2 * count):
        part = pl.ds(i * tile // 2, tile // 2)
        copies.append(pltpu.make_async_copy(w_hbm.at[0, part], w_ref.at[part], sems.at[3 + i]))
    for copy in copies:
        copy.start()
    load = pltpu.make_async_copy(v_hbm.at[0], pack_ref.at[pl.ds(KEYS, KEYS)], sems.at[3 + 2 * count])
    load.start()
    bounds = limits(table_ref, offset_ref)
    pack_ref[2 * KEYS :] = bounds
    fresh_ref[...] = limits(fresh_table_ref, fresh_offset_ref)
    copies[0].wait()
    copies[1].wait()
    part_ref[Q:] = jnp.full((TAIL, WIDE), -1e30, F32)
    for g in range(KV):
        best = masked_scores(g, q_ref[...], pack_ref[:KEYS, g * HD : (g + 1) * HD], bounds, s_ref)
        part_ref[Q + g : Q + g + 1, :ROWS] = best
    load.wait()
    store = pltpu.make_async_copy(pack_ref, pack_hbm, sems.at[4 + 2 * count])
    store.start()
    copies[2].wait()
    grad = split(g_ref[...])
    for i in range(count):
        copies[3 + 2 * i].wait()
        copies[4 + 2 * i].wait()
        part = slice(i * tile, (i + 1) * tile)
        part_ref[:Q, part] = dot3_few(grad, split(w_ref[part]), NT)
    store.wait()


def front(queries, keys, values, grad, w_out, table, offset, fresh_table, fresh_offset):
    hbm, smem, vmem = (pl.BlockSpec(memory_space=m) for m in (pltpu.HBM, pltpu.SMEM, pltpu.VMEM))
    outs = [SCORES, WITH_ROWS, PACK, ((TAIL, KV * HD), F32)]
    return pl.pallas_call(
        front_body,
        out_shape=[jax.ShapeDtypeStruct(s, d) for s, d in outs],
        in_specs=[hbm] * 5 + [smem] * 4,
        out_specs=[vmem, vmem, hbm, vmem],
        scratch_shapes=[
            pltpu.VMEM((Q, WIDE), F32),
            pltpu.VMEM(PACK[0], F32),
            pltpu.VMEM((Q, WIDE), F32),
            pltpu.VMEM((WIDE, WIDE), F32),
            pltpu.SemaphoreType.DMA((11,)),
        ],
        cost_estimate=pl.CostEstimate(flops=0, bytes_accessed=0, transcendentals=0),
        compiler_params=pltpu.CompilerParams(vmem_limit_bytes=FRONT_MB << 20),
    )(queries, keys, values, grad, w_out, table, offset, fresh_table, fresh_offset)


def joined(mine, other):
    first = lax.axis_index("head") % 2 == 0
    return jnp.concatenate([jnp.where(first, mine, other), jnp.where(first, other, mine)], 0)


def dout_body(mine_ref, other_ref, fresh_ref, stats_ref, high_ref, low_ref, *refs):
    part_ref, g_ref = refs[-2:]
    final = lax.axis_index("section") == lax.axis_size("section") - 1
    g = jnp.where(final, fresh_ref[...], joined(mine_ref[...], other_ref[...]))
    g_ref[...] = g
    part_ref[:Q] = dot3_few(split(g), (high_ref[...], low_ref[...]), NT)
    part_ref[Q:] = stats_ref[...]


def dout_second(received, fresh, stats, high, low, *after):
    free = range(6, 6 + len(after))
    return call(dout_body, [WITH_ROWS, FULL], *received, fresh, stats, high, low, *after, free=free)


def split_body(w_ref, *refs):
    high_ref, low_ref = refs[-2:]
    high_ref[...], low_ref[...] = split(w_ref[...])


def split_weights(w, *after):
    return call(split_body, [WEIGHT, WEIGHT], w, *after, free=range(1, 1 + len(after)))


def store_keys(kt_ref, g, k):
    kt_ref[g, :HD], kt_ref[g, HD:] = split(jnp.transpose(k))


def store_values(v_ref, g, v):
    v_ref[:, 2 * g * HD : (2 * g + 1) * HD], v_ref[:, (2 * g + 1) * HD : (2 * g + 2) * HD] = split(v)


def caches_body(k_ref, v_ref, part_ref, kt_ref, v_out, part_out):
    part_out[...] = part_ref[...]
    for g in range(KV):
        cols = slice(g * HD, (g + 1) * HD)
        store_keys(kt_ref, g, k_ref[:, cols])
        store_values(v_out, g, v_ref[:, cols])


def caches(k, v, part):
    return call(caches_body, [KEYS_T, VALUES, WITH_ROWS], k, v, part)


def second_body(q_ref, pack_ref, k_ref, v_ref, bounds_ref, grad_ref, *refs):
    s_ref, top_ref, kt_ref, v_out, copy_ref = refs[-5:]
    final = lax.axis_index("section") == lax.axis_size("section") - 1
    bounds = jnp.where(final, bounds_ref[...], pack_ref[2 * KEYS :])
    top_ref[...] = jnp.full(top_ref.shape, -1e30, F32)
    for g in range(KV):
        cols = slice(g * HD, (g + 1) * HD)
        k = jnp.where(final, k_ref[:, cols], pack_ref[:KEYS, cols])
        top_ref[g : g + 1, :ROWS] = masked_scores(g, q_ref[0, 1], k, bounds, s_ref)
        store_keys(kt_ref, g, k)
        store_values(v_out, g, jnp.where(final, v_ref[:, cols], pack_ref[KEYS : 2 * KEYS, cols]))
    copy_ref[...] = grad_ref[...]


def second(queries, pack, k_fresh, v_fresh, bounds, grad, *after):
    outs = [SCORES, STATS, KEYS_T, VALUES, FULL]
    free = range(6, 6 + len(after))
    return call(second_body, outs, queries, pack, k_fresh, v_fresh, bounds, grad, *after, free=free)


def products_body(d0_ref, d1_ref, s_ref, kt_ref, v_ref, *refs):
    e_ref, dp_ref, a_ref, b_ref, dout_ref = refs[-5:]
    d0, d1 = d0_ref[...], d1_ref[...]
    best = jnp.maximum(d0[Q:], d1[Q:])
    dout = d0[:Q] + d1[:Q]
    dout_ref[...] = dout
    a_ref[Q:] = jnp.zeros((TAIL, WIDE), F32)
    a_groups, b_groups = [], []
    for g in range(KV):
        e = jnp.exp(s_ref[g] - best[g : g + 1, :ROWS])
        e_ref[g] = e
        high, low = split(stacked(dout, g))
        v = v_ref[:, 2 * g * HD : (2 * g + 2) * HD]
        dp = dot(v, jnp.concatenate([high, high], 1), NT) + dot(v[:, :HD], low, NT)
        dp_ref[g] = dp
        total = jnp.sum(e, axis=0, keepdims=True)
        delta = jnp.sum(e * dp, axis=0, keepdims=True)
        mean = jnp.where(total > 0, delta / total, 0.0)
        b = jnp.transpose(key_sum(kt_ref[g], e))
        centred = jnp.transpose(key_sum(kt_ref[g], e * (dp - mean)))
        a_groups.append(centred + as_columns(mean) * b)
        b_groups.append(b)
        a_ref[Q + g : Q + g + 1, :ROWS] = delta
        a_ref[Q + KV + g : Q + KV + g + 1, :ROWS] = total
    a_ref[:Q] = spread(a_groups)
    b_ref[...] = spread(b_groups)


def products(dout, s, kt, v, *after):
    outs = [SCORES, SCORES, WITH_ROWS, FULL, FULL]
    free = range(5, 5 + len(after))
    return call(products_body, outs, *dout, s, kt, v, *after, free=free)


def input_body(step, a0, a1, b0, b1, g_ref, high_ref, low_ref, *refs):
    head = lax.axis_index("head")
    a_all, b_all = a0[...] + a1[...], b0[...] + b1[...]
    refs[-1][...] = a_all[Q:]
    groups = []
    for g in range(KV):
        total = a_all[Q + KV + g : Q + KV + g + 1, :ROWS]
        delta = a_all[Q + g : Q + g + 1, :ROWS] / total
        a, b = stacked(a_all[:Q], g), stacked(b_all, g)
        groups.append((a - as_columns(delta) * b) * as_columns(SCALE / total))
    part = dot3_few(split(spread(groups)), (high_ref[...], low_ref[...]), NT)
    part = part + jnp.where(head == 0, g_ref[...], 0.0)
    if step == 1:
        refs[-2][...] = part
        return
    keep_ref, send_ref = refs[-3:-1]
    first = head % 2 == 0
    keep_ref[...] = jnp.where(first, part[:HALF], part[HALF:])
    send_ref[...] = jnp.where(first, part[HALF:], part[:HALF])


def input_gradient(step, a, b, g, high, low, *after):
    outs = [PIECE, PIECE, STATS] if step == 0 else [FULL, STATS]
    return call(functools.partial(input_body, step), outs, *a, *b, g, high, low, *after, free=range(7, 7 + len(after)))


def sums_body(step, row_ref, e_ref, dp_ref, dout_ref, q_ref, *refs):
    if step == 0:
        key_in, value_in, both_out = refs[0].at[0], refs[1].at[0], refs[-1]
        key_out, value_out = both_out.at[:KEYS], both_out.at[KEYS:]
    else:
        key_in, value_in = refs[0].at[:KEYS], refs[0].at[KEYS:]
        key_out, value_out = refs[-2:]
    for g in range(KV):
        total = row_ref[KV + g : KV + g + 1, :ROWS]
        delta = row_ref[g : g + 1, :ROWS] / total
        probs = e_ref[g] * (1.0 / total)
        d_score = probs * (dp_ref[g] - delta)
        cols = slice(g * HD, (g + 1) * HD)
        value_out[:, cols] = value_in[:, cols] + dot3(split(probs), split(stacked(dout_ref[...], g)), NN)
        q = split(stacked(q_ref[0, step], g))
        key_out[:, cols] = key_in[:, cols] + SCALE * dot3(split(d_score), q, NN)


def gradient_sums(step, rows, e, dp, dout, queries, sums, *after):
    outs = [((2 * KEYS, KV * HD), F32)] if step == 0 else [CACHE, CACHE]
    count = 5 + len(sums)
    free = range(count, count + len(after))
    return call(functools.partial(sums_body, step), outs, rows, e, dp, dout, queries, *sums, *after, free=free)


def swap(bits, n=4):
    return [(i, i ^ bits) for i in range(n)]


def neighbours(turn):
    return [(h * 4 + p, h * 4 + (p ^ (1 if (h + turn) % 2 == 0 else 3))) for h in range(4) for p in range(4)]


def page_sum(x, join=jnp.add, held=None, turn=0):
    x = join(x if held is None else held, lax.ppermute(x, ("head", "page"), neighbours(turn)))
    return x, lax.ppermute(x, ("head", "page"), neighbours(turn + 1))


def sum_and_top(a, b):
    rows = lax.broadcasted_iota(jnp.int32, a.shape, 0)
    return jnp.where(rows < Q, a + b, jnp.maximum(a, b))


def tied(value, after):
    return lax.optimization_barrier((value, after))[0]


def per_device(
    grad_in, grad_fresh, queries, key_cache, value_cache, key_fresh, value_fresh, key_grad_in, value_grad_in,
    page_table, offsets, page_fresh, offset_fresh, w_query, w_out,
):
    back_section = [(i, i - 1) for i in range(1, 16)]

    s1, part, pack, fresh_bounds = front(
        queries, key_cache, value_cache, grad_in, w_out, page_table[0], offsets, page_fresh, offset_fresh
    )
    *split1, near = caches(key_cache[0], value_cache[0], part)
    dout1 = page_sum(part, sum_and_top, near)
    wq_high, wq_low = split_weights(w_query[0], dout1[0])
    pack2 = lax.ppermute(pack, "section", back_section)
    e1, dp1, a, b, dout1 = products(dout1, s1, *split1, wq_high)
    a1, b1 = page_sum(a), page_sum(b, turn=1)
    wo_high, wo_low = split_weights(w_out[0], a1[0])
    keep, send, rows1 = input_gradient(0, a1, b1, grad_in[0], wq_high, wq_low, wo_high)
    part = keep + lax.ppermute(send, "head", swap(1))
    (sums,) = gradient_sums(0, rows1, e1, dp1, dout1, queries, (key_grad_in, value_grad_in), part)
    part = part + lax.ppermute(part, "head", swap(2))
    mine = lax.ppermute(tied(part, sums), "section", back_section)
    s2, m2, *split2, fresh = second(queries, pack2, key_fresh, value_fresh, fresh_bounds, grad_fresh, part)
    mine = tied(mine, m2)
    other = lax.ppermute(mine, "head", swap(1))

    part, g2 = dout_second((mine, other), fresh, m2, wo_high, wo_low, sums)
    dout2 = page_sum(part, sum_and_top)
    sums = lax.ppermute(tied(sums, m2), "section", back_section)
    e2, dp2, a, b, dout2 = products(dout2, s2, *split2)
    a2, b2 = page_sum(a), page_sum(b, lambda x, y: tied(x + y, sums), turn=1)
    part, rows2 = input_gradient(1, a2, b2, g2, wq_high, wq_low)
    part = part + lax.ppermute(part, "head", swap(1))
    key_final, value_final = gradient_sums(1, rows2, e2, dp2, dout2, queries, (sums,), part)
    grad_done = part + tied(lax.ppermute(part, "head", swap(2)), key_final)
    return (grad_done[None], key_final[None], value_final[None])


def solution(mesh):
    placed = (
        P("section", None, "page"),
        P(None, "page"),
        P("section", None, None, "head"),
        P("section", "page", "head"),
        P("section", "page", "head"),
        P("page", "head"),
        P("page", "head"),
        P("section", "page", "head"),
        P("section", "page", "head"),
        P("section", None),
        P("section"),
        P(),
        P(),
        P("section", "page", "head"),
        P("section", "head", "page"),
    )
    return jax.shard_map(
        per_device,
        mesh=mesh,
        in_specs=placed,
        out_specs=(
            P("section", None, "page"),
            P("section", "page", "head"),
            P("section", "page", "head"),
        ),
        check_vma=False,
    )
```

```python
import functools

import jax
import jax.numpy as jnp
from jax import lax
from jax.experimental import pallas as pl
from jax.experimental.pallas import tpu as pltpu
from jax.sharding import PartitionSpec as P

HD = 128
BLOCK = 128
Q = 64
HALF = Q // 2
FRONT_MB = 60
TAIL = 8
KEYS = 512
KV = 2
GROUP = 3
ROWS = GROUP * Q
WIDE = KV * GROUP * HD
SCALE = HD ** (-0.5)
F32 = jnp.float32
BF16 = jnp.bfloat16
NN = (((1,), (0,)), ((), ()))
NT = (((1,), (1,)), ((), ()))


def split(x):
    high = x.astype(BF16)
    return high, (x - high.astype(F32)).astype(BF16)


def dot(a, b, dims):
    return lax.dot_general(a, b, dims, preferred_element_type=F32)


def dot3(a, b, dims):
    (a_high, a_low), (b_high, b_low) = a, b
    return dot(a_high, b_high, dims) + (dot(a_low, b_high, dims) + dot(a_high, b_low, dims))


def dot3_few(a, b, dims):
    (a_high, a_low), (b_high, b_low) = a, b
    rows = a_high.shape[0]
    both = dot(jnp.concatenate([a_high, a_low], 0), b_high, dims)
    return both[:rows] + (both[rows:] + dot(a_high, b_low, dims))


def key_sum(kt, x):
    high, low = split(x)
    both = dot(kt, high, NN)
    return both[:HD] + (both[HD:] + dot(kt[:HD], low, NN))


def stacked(x, g):
    return jnp.concatenate([x[:, (g * GROUP + r) * HD : (g * GROUP + r + 1) * HD] for r in range(GROUP)], 0)


def spread(groups):
    return jnp.concatenate([groups[g][r * Q : (r + 1) * Q] for g in range(KV) for r in range(GROUP)], 1)


def as_columns(row):
    return jnp.transpose(jnp.broadcast_to(row, (HD, ROWS)))


def call(body, outs, *args, scratch=(), mb=6, smem=(), free=()):
    spaces = [pltpu.SMEM if i in smem else pl.ANY if i in free else pltpu.VMEM for i in range(len(args))]
    return pl.pallas_call(
        body,
        out_shape=[jax.ShapeDtypeStruct(s, d) for s, d in outs],
        in_specs=[pl.BlockSpec(memory_space=space) for space in spaces],
        out_specs=[pl.BlockSpec(memory_space=pltpu.VMEM)] * len(outs),
        scratch_shapes=scratch,
        cost_estimate=pl.CostEstimate(flops=0, bytes_accessed=0, transcendentals=0),
        compiler_params=pltpu.CompilerParams(vmem_limit_bytes=mb << 20),
    )(*args)


SCORES = ((KV, KEYS, ROWS), F32)
CACHE = ((KEYS, KV * HD), F32)
FULL = ((Q, WIDE), F32)
PIECE = ((HALF, WIDE), F32)
WITH_ROWS = ((Q + TAIL, WIDE), F32)
STATS = ((TAIL, WIDE), F32)
PACK = ((2 * KEYS + TAIL, KV * HD), F32)
WEIGHT = ((WIDE, WIDE), BF16)
KEYS_T = ((KV, 2 * HD, KEYS), BF16)
VALUES = ((KEYS, 2 * KV * HD), BF16)


def limits(table_ref, offset_ref):
    page = lax.axis_index("page")
    rows = []
    for b in range(8):
        bound = offset_ref[0] - table_ref[page * 4 + b % 4] * BLOCK
        rows.append(jnp.full((1, KV * HD), bound, jnp.int32).astype(F32))
    return jnp.concatenate(rows, 0)


def masked_scores(g, q, k, bounds, s_ref):
    lead = (
        lax.broadcasted_iota(jnp.int32, (BLOCK, ROWS), 0) - lax.broadcasted_iota(jnp.int32, (BLOCK, ROWS), 1) % Q
    ).astype(F32)
    s = lax.dot_general(
        k, stacked(q, g), NT, precision=lax.Precision.HIGHEST, preferred_element_type=F32
    ) * SCALE
    best = None
    for b in range(KEYS // BLOCK):
        block = jnp.where(lead <= bounds[b : b + 1, :ROWS], s[b * BLOCK : (b + 1) * BLOCK], -1e30)
        s_ref[g, b * BLOCK : (b + 1) * BLOCK] = block
        most = jnp.max(block, axis=0, keepdims=True)
        best = most if best is None else jnp.maximum(best, most)
    return best


def front_body(
    q_hbm, k_hbm, v_hbm, g_hbm, w_hbm, table_ref, offset_ref, fresh_table_ref, fresh_offset_ref,
    s_ref, part_ref, pack_hbm, fresh_ref,
    q_ref, pack_ref, g_ref, w_ref, sems,
):
    count = 3
    tile = WIDE // count
    copies = [
        pltpu.make_async_copy(q_hbm.at[0, 0], q_ref, sems.at[0]),
        pltpu.make_async_copy(k_hbm.at[0], pack_ref.at[pl.ds(0, KEYS)], sems.at[1]),
        pltpu.make_async_copy(g_hbm.at[0], g_ref, sems.at[2]),
    ]
    for i in range(2 * count):
        part = pl.ds(i * tile // 2, tile // 2)
        copies.append(pltpu.make_async_copy(w_hbm.at[0, part], w_ref.at[part], sems.at[3 + i]))
    for copy in copies:
        copy.start()
    load = pltpu.make_async_copy(v_hbm.at[0], pack_ref.at[pl.ds(KEYS, KEYS)], sems.at[3 + 2 * count])
    load.start()
    bounds = limits(table_ref, offset_ref)
    pack_ref[2 * KEYS :] = bounds
    fresh_ref[...] = limits(fresh_table_ref, fresh_offset_ref)
    copies[0].wait()
    copies[1].wait()
    part_ref[Q:] = jnp.full((TAIL, WIDE), -1e30, F32)
    for g in range(KV):
        best = masked_scores(g, q_ref[...], pack_ref[:KEYS, g * HD : (g + 1) * HD], bounds, s_ref)
        part_ref[Q + g : Q + g + 1, :ROWS] = best
    load.wait()
    store = pltpu.make_async_copy(pack_ref, pack_hbm, sems.at[4 + 2 * count])
    store.start()
    copies[2].wait()
    grad = split(g_ref[...])
    for i in range(count):
        copies[3 + 2 * i].wait()
        copies[4 + 2 * i].wait()
        part = slice(i * tile, (i + 1) * tile)
        part_ref[:Q, part] = dot3_few(grad, split(w_ref[part]), NT)
    store.wait()


def front(queries, keys, values, grad, w_out, table, offset, fresh_table, fresh_offset):
    hbm, smem, vmem = (pl.BlockSpec(memory_space=m) for m in (pltpu.HBM, pltpu.SMEM, pltpu.VMEM))
    outs = [SCORES, WITH_ROWS, PACK, ((TAIL, KV * HD), F32)]
    return pl.pallas_call(
        front_body,
        out_shape=[jax.ShapeDtypeStruct(s, d) for s, d in outs],
        in_specs=[hbm] * 5 + [smem] * 4,
        out_specs=[vmem, vmem, hbm, vmem],
        scratch_shapes=[
            pltpu.VMEM((Q, WIDE), F32),
            pltpu.VMEM(PACK[0], F32),
            pltpu.VMEM((Q, WIDE), F32),
            pltpu.VMEM((WIDE, WIDE), F32),
            pltpu.SemaphoreType.DMA((11,)),
        ],
        cost_estimate=pl.CostEstimate(flops=0, bytes_accessed=0, transcendentals=0),
        compiler_params=pltpu.CompilerParams(vmem_limit_bytes=FRONT_MB << 20),
    )(queries, keys, values, grad, w_out, table, offset, fresh_table, fresh_offset)


def joined(mine, other):
    first = lax.axis_index("head") % 2 == 0
    return jnp.concatenate([jnp.where(first, mine, other), jnp.where(first, other, mine)], 0)


def dout_body(mine_ref, other_ref, fresh_ref, stats_ref, high_ref, low_ref, *refs):
    part_ref, g_ref = refs[-2:]
    final = lax.axis_index("section") == lax.axis_size("section") - 1
    g = jnp.where(final, fresh_ref[...], joined(mine_ref[...], other_ref[...]))
    g_ref[...] = g
    part_ref[:Q] = dot3_few(split(g), (high_ref[...], low_ref[...]), NT)
    part_ref[Q:] = stats_ref[...]


def dout_second(received, fresh, stats, high, low, *after):
    free = range(6, 6 + len(after))
    return call(dout_body, [WITH_ROWS, FULL], *received, fresh, stats, high, low, *after, free=free)


def split_body(w_ref, *refs):
    high_ref, low_ref = refs[-2:]
    high_ref[...], low_ref[...] = split(w_ref[...])


def split_weights(w, *after):
    return call(split_body, [WEIGHT, WEIGHT], w, *after, free=range(1, 1 + len(after)))


def store_keys(kt_ref, g, k):
    kt_ref[g, :HD], kt_ref[g, HD:] = split(jnp.transpose(k))


def store_values(v_ref, g, v):
    v_ref[:, 2 * g * HD : (2 * g + 1) * HD], v_ref[:, (2 * g + 1) * HD : (2 * g + 2) * HD] = split(v)


def caches_body(k_ref, v_ref, part_ref, kt_ref, v_out, part_out):
    part_out[...] = part_ref[...]
    for g in range(KV):
        cols = slice(g * HD, (g + 1) * HD)
        store_keys(kt_ref, g, k_ref[:, cols])
        store_values(v_out, g, v_ref[:, cols])


def caches(k, v, part):
    return call(caches_body, [KEYS_T, VALUES, WITH_ROWS], k, v, part)


def second_body(q_ref, pack_ref, k_ref, v_ref, bounds_ref, grad_ref, *refs):
    s_ref, top_ref, kt_ref, v_out, copy_ref = refs[-5:]
    final = lax.axis_index("section") == lax.axis_size("section") - 1
    bounds = jnp.where(final, bounds_ref[...], pack_ref[2 * KEYS :])
    top_ref[...] = jnp.full(top_ref.shape, -1e30, F32)
    for g in range(KV):
        cols = slice(g * HD, (g + 1) * HD)
        k = jnp.where(final, k_ref[:, cols], pack_ref[:KEYS, cols])
        top_ref[g : g + 1, :ROWS] = masked_scores(g, q_ref[0, 1], k, bounds, s_ref)
        store_keys(kt_ref, g, k)
        store_values(v_out, g, jnp.where(final, v_ref[:, cols], pack_ref[KEYS : 2 * KEYS, cols]))
    copy_ref[...] = grad_ref[...]


def second(queries, pack, k_fresh, v_fresh, bounds, grad, *after):
    outs = [SCORES, STATS, KEYS_T, VALUES, FULL]
    free = range(6, 6 + len(after))
    return call(second_body, outs, queries, pack, k_fresh, v_fresh, bounds, grad, *after, free=free)


def products_body(d0_ref, d1_ref, s_ref, kt_ref, v_ref, *refs):
    e_ref, dp_ref, a_ref, b_ref, dout_ref = refs[-5:]
    d0, d1 = d0_ref[...], d1_ref[...]
    best = jnp.maximum(d0[Q:], d1[Q:])
    dout = d0[:Q] + d1[:Q]
    dout_ref[...] = dout
    a_ref[Q:] = jnp.zeros((TAIL, WIDE), F32)
    a_groups, b_groups = [], []
    for g in range(KV):
        e = jnp.exp(s_ref[g] - best[g : g + 1, :ROWS])
        e_ref[g] = e
        high, low = split(stacked(dout, g))
        v = v_ref[:, 2 * g * HD : (2 * g + 2) * HD]
        dp = dot(v, jnp.concatenate([high, high], 1), NT) + dot(v[:, :HD], low, NT)
        dp_ref[g] = dp
        total = jnp.sum(e, axis=0, keepdims=True)
        delta = jnp.sum(e * dp, axis=0, keepdims=True)
        mean = jnp.where(total > 0, delta / total, 0.0)
        b = jnp.transpose(key_sum(kt_ref[g], e))
        centred = jnp.transpose(key_sum(kt_ref[g], e * (dp - mean)))
        a_groups.append(centred + as_columns(mean) * b)
        b_groups.append(b)
        a_ref[Q + g : Q + g + 1, :ROWS] = delta
        a_ref[Q + KV + g : Q + KV + g + 1, :ROWS] = total
    a_ref[:Q] = spread(a_groups)
    b_ref[...] = spread(b_groups)


def products(dout, s, kt, v, *after):
    outs = [SCORES, SCORES, WITH_ROWS, FULL, FULL]
    free = range(5, 5 + len(after))
    return call(products_body, outs, *dout, s, kt, v, *after, free=free)


def input_body(step, a0, a1, b0, b1, g_ref, high_ref, low_ref, *refs):
    head = lax.axis_index("head")
    a_all, b_all = a0[...] + a1[...], b0[...] + b1[...]
    refs[-1][...] = a_all[Q:]
    groups = []
    for g in range(KV):
        total = a_all[Q + KV + g : Q + KV + g + 1, :ROWS]
        delta = a_all[Q + g : Q + g + 1, :ROWS] / total
        a, b = stacked(a_all[:Q], g), stacked(b_all, g)
        groups.append((a - as_columns(delta) * b) * as_columns(SCALE / total))
    part = dot3_few(split(spread(groups)), (high_ref[...], low_ref[...]), NT)
    part = part + jnp.where(head == 0, g_ref[...], 0.0)
    if step == 1:
        refs[-2][...] = part
        return
    keep_ref, send_ref = refs[-3:-1]
    first = head % 2 == 0
    keep_ref[...] = jnp.where(first, part[:HALF], part[HALF:])
    send_ref[...] = jnp.where(first, part[HALF:], part[:HALF])


def input_gradient(step, a, b, g, high, low, *after):
    outs = [PIECE, PIECE, STATS] if step == 0 else [FULL, STATS]
    return call(functools.partial(input_body, step), outs, *a, *b, g, high, low, *after, free=range(7, 7 + len(after)))


def sums_body(step, row_ref, e_ref, dp_ref, dout_ref, q_ref, *refs):
    if step == 0:
        key_in, value_in, both_out = refs[0].at[0], refs[1].at[0], refs[-1]
        key_out, value_out = both_out.at[:KEYS], both_out.at[KEYS:]
    else:
        key_in, value_in = refs[0].at[:KEYS], refs[0].at[KEYS:]
        key_out, value_out = refs[-2:]
    for g in range(KV):
        total = row_ref[KV + g : KV + g + 1, :ROWS]
        delta = row_ref[g : g + 1, :ROWS] / total
        probs = e_ref[g] * (1.0 / total)
        d_score = probs * (dp_ref[g] - delta)
        cols = slice(g * HD, (g + 1) * HD)
        value_out[:, cols] = value_in[:, cols] + dot3(split(probs), split(stacked(dout_ref[...], g)), NN)
        q = split(stacked(q_ref[0, step], g))
        key_out[:, cols] = key_in[:, cols] + SCALE * dot3(split(d_score), q, NN)


def gradient_sums(step, rows, e, dp, dout, queries, sums, *after):
    outs = [((2 * KEYS, KV * HD), F32)] if step == 0 else [CACHE, CACHE]
    count = 5 + len(sums)
    free = range(count, count + len(after))
    return call(functools.partial(sums_body, step), outs, rows, e, dp, dout, queries, *sums, *after, free=free)


def swap(bits, n=4):
    return [(i, i ^ bits) for i in range(n)]


def neighbours(turn):
    return [(h * 4 + p, h * 4 + (p ^ (1 if (h + turn) % 2 == 0 else 3))) for h in range(4) for p in range(4)]


def page_sum(x, join=jnp.add, held=None, turn=0):
    x = join(x if held is None else held, lax.ppermute(x, ("head", "page"), neighbours(turn)))
    return x, lax.ppermute(x, ("head", "page"), neighbours(turn + 1))


def page_sum_halves(x, join, held=None):
    half = WIDE // 2
    parts = []
    for turn in (0, 1):
        cols = slice(turn * half, (turn + 1) * half)
        parts.append(page_sum(x[:, cols], join, None if held is None else held[:, cols], turn))
    return [jnp.concatenate([left, right], 1) for left, right in zip(*parts)]


def sum_and_top(a, b):
    rows = lax.broadcasted_iota(jnp.int32, a.shape, 0)
    return jnp.where(rows < Q, a + b, jnp.maximum(a, b))


def tied(value, after):
    return lax.optimization_barrier((value, after))[0]


def per_device(
    grad_in, grad_fresh, queries, key_cache, value_cache, key_fresh, value_fresh, key_grad_in, value_grad_in,
    page_table, offsets, page_fresh, offset_fresh, w_query, w_out,
):
    back_section = [(i, i - 1) for i in range(1, 16)]

    s1, part, pack, fresh_bounds = front(
        queries, key_cache, value_cache, grad_in, w_out, page_table[0], offsets, page_fresh, offset_fresh
    )
    *split1, near = caches(key_cache[0], value_cache[0], part)
    dout1 = page_sum_halves(part, sum_and_top, near)
    wq_high, wq_low = split_weights(w_query[0], dout1[0])
    pack2 = lax.ppermute(pack, "section", back_section)
    e1, dp1, a, b, dout1 = products(dout1, s1, *split1, wq_high)
    a1, b1 = page_sum(a), page_sum(b, turn=1)
    wo_high, wo_low = split_weights(w_out[0], a1[0])
    keep, send, rows1 = input_gradient(0, a1, b1, grad_in[0], wq_high, wq_low, wo_high)
    part = keep + lax.ppermute(send, "head", swap(1))
    (sums,) = gradient_sums(0, rows1, e1, dp1, dout1, queries, (key_grad_in, value_grad_in), part)
    part = part + lax.ppermute(part, "head", swap(2))
    mine = lax.ppermute(tied(part, sums), "section", back_section)
    s2, m2, *split2, fresh = second(queries, pack2, key_fresh, value_fresh, fresh_bounds, grad_fresh, part)
    mine = tied(mine, m2)
    other = lax.ppermute(mine, "head", swap(1))

    part, g2 = dout_second((mine, other), fresh, m2, wo_high, wo_low, sums)
    dout2 = page_sum_halves(part, sum_and_top)
    sums = lax.ppermute(tied(sums, m2), "section", back_section)
    e2, dp2, a, b, dout2 = products(dout2, s2, *split2)
    a2, b2 = page_sum(a), page_sum(b, lambda x, y: tied(x + y, sums), turn=1)
    part, rows2 = input_gradient(1, a2, b2, g2, wq_high, wq_low)
    part = part + lax.ppermute(part, "head", swap(1))
    key_final, value_final = gradient_sums(1, rows2, e2, dp2, dout2, queries, (sums,), part)
    grad_done = part + tied(lax.ppermute(part, "head", swap(2)), key_final)
    return (grad_done[None], key_final[None], value_final[None])


def solution(mesh):
    placed = (
        P("section", None, "page"),
        P(None, "page"),
        P("section", None, None, "head"),
        P("section", "page", "head"),
        P("section", "page", "head"),
        P("page", "head"),
        P("page", "head"),
        P("section", "page", "head"),
        P("section", "page", "head"),
        P("section", None),
        P("section"),
        P(),
        P(),
        P("section", "page", "head"),
        P("section", "head", "page"),
    )
    return jax.shard_map(
        per_device,
        mesh=mesh,
        in_specs=placed,
        out_specs=(
            P("section", None, "page"),
            P("section", "page", "head"),
            P("section", "page", "head"),
        ),
        check_vma=False,
    )
```
